256 devices in a mesh: cols: 16 (over z_lo, y, core), cells: 16 (over x, z_hi).
Axes of the slice: x: 4, y: 4, z: 8 (z_hi: 4, z_lo: 2; z = z_hi * 2 + z_lo), core: 2. Of those that a mesh axis runs over, the one named last changes fastest.
Arguments:
- slab_cols: float32 [1024, 131072], P('cols', 'cells'), may hold values from -6 to 6
- observed_cov: float32 [2, 16, 131072], P(None, 'cols', 'cells'), may hold values from -1 to 30, as said below
- observed_cells: int32 [2, 16], replicated, may hold values from 0 to 131071, as said below
- noise_variance: float32 [2, 16], replicated, may hold values from 1 to 8
- wind_across: float32 [256, 512], P('cells'), may hold values from 0.25 to 0.5
- wind_along: float32 [256, 512], P('cells'), may hold values from -0.3 to 0.3
- diffusion: float32 [256, 512], P('cells'), may hold values from 0.125 to 0.25
Outputs:
- forecast: float32 [1024, 131072], P('cols', 'cells')
The draws below stay inside these ranges and needn't reach their ends.
Inputs may be any that keep to these rules, and one draw needn't show every extreme that they name: `observed_cells`: the 32 observed cells are all different, so the two updates observe different cells. observed_cov[u, k, observed_cells[u, k]] lies between 20 and 30; every other entry lies between -1 and 1.
All inputs are finite; a program needn't handle non-finite values.
Results may differ from the reference program's by a relative error of at most 0.00012.
Values sent between devices are 32-bit elements; how exact they have to be, the bound alone decides.
A program may use at most 64 MiB of HBM per device.

```python
import math
import jax
import jax.numpy as jnp
from jax import lax

GY = 512
K = 16
SECTIONS = 8
SLAB = 1024
GX = 256
NCELL = 131072


def chosen_cells(key):
    shuffled = jax.random.permutation(jax.random.fold_in(key, 7), NCELL)
    return shuffled[:2 * K].reshape(2, K).astype(jnp.int32)


def draw_observed_cells(key, part):
    return chosen_cells(key)


def draw_observed_cov(key, part):
    cells = chosen_cells(key)
    all_cells = cells.reshape(2 * K)
    entries = jax.random.uniform(jax.random.fold_in(key, 11), (2, K, NCELL), jnp.float32, -1.0, 1.0)
    coherent = jax.random.uniform(jax.random.fold_in(key, 19), (2, K, 2 * K), jnp.float32, 0.6, 1.0)
    entries = entries.at[:, :, all_cells].set(coherent)
    variance = jax.random.uniform(jax.random.fold_in(key, 13), (2, K), jnp.float32, 20.0, 30.0)
    update_ids = jnp.arange(2)[:, None]
    row_ids = jnp.arange(K)[None, :]
    return entries.at[update_ids, row_ids, cells].set(variance)


def draw_slab_cols(key, part):
    all_cells = chosen_cells(key).reshape(2 * K)
    entries = jax.random.truncated_normal(jax.random.fold_in(key, 21), -6.0, 6.0, (SLAB, NCELL), jnp.float32)
    picked = jax.random.uniform(jax.random.fold_in(key, 23), (SLAB, 2 * K), jnp.float32, 4.0, 6.0)
    return entries.at[:, all_cells].set(picked)


def level_of(rng, extent, shards, low, high):
    loudness = 1.0
    for dim, shards_of in shards:
        draws = jax.random.uniform(jax.random.fold_in(jax.random.fold_in(rng, 6), dim), (shards_of,), jnp.float32, low / len(shards), high / len(shards))
        loudness = loudness * jnp.repeat(jnp.exp(draws), extent[dim] // shards_of).reshape((-1,) + (1,) * (len(extent) - 1 - dim))
    return loudness


def setup_inputs(seed: int = 0) -> dict:
    streams_of = jax.random.split(jax.random.key(seed), 8)
    slab_cols = draw_slab_cols(jax.random.fold_in(streams_of[7], 71), 0)
    observed_cov = draw_observed_cov(jax.random.fold_in(streams_of[7], 71), 0)
    observed_cells = draw_observed_cells(jax.random.fold_in(streams_of[7], 71), 0)
    noise_variance = jnp.clip(jnp.exp(jax.random.uniform(streams_of[3], (2, K), jnp.float32, math.log(1.0), math.log(8.0))), 1.0, 8.0)
    wind_across = jnp.clip(0.25 + 0.25 * jax.random.uniform(streams_of[4], (GX, GY), jnp.float32) ** level_of(streams_of[4], (GX, GY), ((0, 16),), -0.2, 0.2), 0.25, 0.5)
    wind_along = jnp.clip(jax.random.uniform(streams_of[5], (GX, GY), jnp.float32, -0.3, 0.3) * level_of(streams_of[5], (GX, GY), ((0, 16),), -0.4, 0.0), -0.3, 0.3)
    diffusion = jnp.clip(0.125 + 0.125 * jax.random.uniform(streams_of[6], (GX, GY), jnp.float32) ** level_of(streams_of[6], (GX, GY), ((0, 16),), -0.2, 0.2), 0.125, 0.25)
    return {"slab_cols": slab_cols, "observed_cov": observed_cov, "observed_cells": observed_cells, "noise_variance": noise_variance, "wind_across": wind_across, "wind_along": wind_along, "diffusion": diffusion}


def invert_small(matrix):
    dimension = matrix.shape[0]
    joined = jnp.concatenate([matrix, jnp.eye(dimension, dtype=matrix.dtype)], axis=1)
    for column in range(dimension):
        scaled = joined[column] / joined[column, column]
        joined = joined - joined[:, column:column + 1] * scaled[None, :]
        joined = joined.at[column].set(scaled)
    return joined[:, dimension:]


def symmetric(block):
    return 0.5 * (block + block.T)


def product(left, right):
    return jnp.dot(left, right, precision=lax.Precision.HIGHEST, preferred_element_type=jnp.float32)


def advance(field, across, along, spread):
    above_row = jnp.roll(field, -1, axis=1)
    below_row = jnp.roll(field, 1, axis=1)
    east_cell = jnp.roll(field, -1, axis=2)
    west_cell = jnp.roll(field, 1, axis=2)
    return field - 0.5 * across * (above_row - below_row) - 0.5 * along * (east_cell - west_cell) + spread * (above_row + below_row + east_cell + west_cell - 4.0 * field)


def reference(slab_cols, observed_cov, observed_cells, noise_variance, wind_across, wind_along, diffusion):
    first_cells = observed_cells[0]
    second_cells = observed_cells[1]
    first_cov = observed_cov[0]
    second_cov = observed_cov[1]
    first_block = first_cov[:, first_cells]
    cross_block = first_cov[:, second_cells]
    second_block = second_cov[:, second_cells]
    first_matrix = symmetric(first_block) + jnp.diag(noise_variance[0])
    first_inverse = invert_small(first_matrix)
    first_gain = product(first_inverse, first_cov)
    updated = slab_cols - product(slab_cols[:, first_cells], first_gain)
    revised_cov = second_cov - product(cross_block.T, first_gain)
    revised_block = revised_cov[:, second_cells]
    second_matrix = symmetric(revised_block) + jnp.diag(noise_variance[1])
    second_gain = product(invert_small(second_matrix), revised_cov)
    analysis = updated - product(updated[:, second_cells], second_gain)
    field = analysis.reshape(analysis.shape[0], GX, GY)
    for number in range(SECTIONS):
        field = advance(field, wind_across, wind_along, diffusion)
    return field.reshape(analysis.shape[0], NCELL)
```

```python
import jax
import jax.numpy as jnp
from jax import lax
from jax.experimental import pallas as pl
from jax.experimental.pallas import tpu as pltpu
from jax.sharding import PartitionSpec as P

SECTIONS = 8
GROUP = 8
LANES = 128
AHEAD = 3
MESH = pl.DeviceIdType.MESH


def place(k):
    return (k % 2) * 8 + ((k // 2) % 4) * 2 + k // 8


def kernel(
    cells_ref, noise_ref, slab_ref, cov_ref, across_ref, along_ref, spread_ref, out_ref,
    own, low, high, flat, head, natural, coef, buf_a, buf_b, gathered, corr, result, weight,
    msg_x, slots_x, msg_z, slots_z, msg_c, slots_c,
    local_sem, out_sem, halo_send, halo_recv, head_send, head_recv,
    x_send, x_recv, z_send, z_recv, c_send, c_recv,
    pair_send, pair_recv, y_send, y_recv, core_send, core_recv,
):
    columns, local_cells = slab_ref.shape
    grid_rows, width = across_ref.shape
    count = cells_ref.shape[1]
    total = 2 * count
    groups = columns // GROUP
    edge = SECTIONS * width
    extent = grid_rows + 2 * SECTIONS

    c = lax.axis_index("cols")
    t = lax.axis_index("cells")
    core, y, z_lo = lax.rem(c, 2), lax.rem(lax.div(c, 2), 4), lax.div(c, 8)
    x, z_hi = lax.div(t, 4), lax.rem(t, 4)
    mine = core * 8 + y * 2 + z_lo
    after, before = lax.rem(t + 1, 16), lax.rem(t + 15, 16)

    def cells_device(target):
        return {"cells": target}

    def cols_device(target):
        return {"cols": target}

    def remote(src, dst, send, recv, device):
        return pltpu.make_async_remote_copy(
            src_ref=src, dst_ref=dst, send_sem=send, recv_sem=recv, device_id=device, device_id_type=MESH
        )

    x_peers = [lax.rem(x + d, 4) for d in range(1, 4)]
    z_peers = [lax.rem(z_hi + d, 4) for d in range(1, 4)]
    c_peers = [lax.rem(c + d, 16) for d in range(1, 16)]
    y_peers = [lax.rem(y + d, 4) for d in range(1, 4)]

    locals_ = [
        pltpu.make_async_copy(cov_ref, flat, local_sem.at[0]),
        pltpu.make_async_copy(across_ref, head.at[0, SECTIONS : SECTIONS + grid_rows], local_sem.at[1]),
        pltpu.make_async_copy(along_ref, head.at[1, SECTIONS : SECTIONS + grid_rows], local_sem.at[2]),
        pltpu.make_async_copy(spread_ref, head.at[2, SECTIONS : SECTIONS + grid_rows], local_sem.at[3]),
        pltpu.make_async_copy(slab_ref, own, local_sem.at[4]),
    ]
    for copy in locals_:
        copy.start()

    barrier = pltpu.get_barrier_semaphore()
    peers = (
        [cells_device(after), cells_device(before)]
        + [cells_device(p * 4 + z_hi) for p in x_peers]
        + [cells_device(x * 4 + p) for p in z_peers]
        + [cols_device(p) for p in c_peers]
    )
    for device in peers:
        pl.semaphore_signal(barrier, inc=1, device_id=device, device_id_type=MESH)

    for copy in locals_[:4]:
        copy.wait()
    for u in range(2):
        for i in range(grid_rows):
            head[3 + u, SECTIONS + i : SECTIONS + i + 1, :] = flat[u, :, i * width : (i + 1) * width]
    pl.semaphore_wait(barrier, len(peers))

    top = SECTIONS + grid_rows
    head_up = remote(
        head.at[:, grid_rows : grid_rows + SECTIONS, :], head.at[:, 0:SECTIONS, :],
        head_send.at[0], head_recv.at[0], cells_device(after),
    )
    head_down = remote(
        head.at[:, SECTIONS : 2 * SECTIONS, :], head.at[:, top : top + SECTIONS, :],
        head_send.at[1], head_recv.at[1], cells_device(before),
    )
    head_up.start()
    head_down.start()

    def halos(g):
        rows = pl.ds(pl.multiple_of(g * GROUP, GROUP), GROUP)
        return (
            remote(
                slab_ref.at[rows, local_cells - edge : local_cells], low.at[rows, :],
                halo_send.at[0, g], halo_recv.at[0, g], cells_device(after),
            ),
            remote(
                slab_ref.at[rows, 0:edge], high.at[rows, :],
                halo_send.at[1, g], halo_recv.at[1, g], cells_device(before),
            ),
        )

    for g in range(AHEAD):
        for copy in halos(g):
            copy.start()

    locals_[4].wait()
    part = 2 * width
    row_q = lax.broadcasted_iota(jnp.int32, (total, LANES), 0)
    wanted = jnp.zeros((total, LANES), jnp.int32)
    for u in range(2):
        for k in range(count):
            wanted = jnp.where(row_q == place(k) * 2 + u, cells_ref[u, k], wanted)
    wanted = jnp.concatenate([wanted] * (part // LANES), axis=1) - t * local_cells
    lane = lax.broadcasted_iota(jnp.int32, (total, part), 1)
    sub_8 = lax.broadcasted_iota(jnp.int32, (GROUP, part), 0)
    first_row = 2 * lax.rem(mine, 4)
    bf16 = jnp.bfloat16

    def pick(n, found):
        start = pl.multiple_of(n * part, part)
        chosen = jnp.where(lane + start == wanted, 1.0, 0.0).astype(bf16)
        rows = jnp.where(
            sub_8 == first_row,
            flat[0, :, pl.ds(start, part)],
            jnp.where(sub_8 == first_row + 1, flat[1, :, pl.ds(start, part)], 0.0),
        )
        block = jnp.concatenate([own[:, pl.ds(start, part)], rows, jnp.zeros_like(rows)], axis=0)
        upper = block.astype(bf16)
        rest = block - upper.astype(jnp.float32)
        middle = rest.astype(bf16)
        lower = (rest - middle.astype(jnp.float32)).astype(bf16)
        pieces = jnp.concatenate([upper, middle, lower], axis=0)
        return found + lax.dot_general(
            pieces, chosen, (((1,), (1,)), ((), ())), preferred_element_type=jnp.float32
        )

    height = columns + 2 * GROUP
    found = lax.fori_loop(
        0, local_cells // part, pick, jnp.zeros((3 * height, total), jnp.float32)
    )
    found = found[0:height] + found[height : 2 * height] + found[2 * height : 3 * height]
    found = jnp.concatenate([found, jnp.zeros((height, LANES - total), jnp.float32)], axis=1)
    square = jnp.concatenate(
        [
            jnp.zeros((total, LANES), jnp.float32),
            found[0:columns],
            jnp.zeros((LANES - total - columns, LANES), jnp.float32),
        ],
        axis=0,
    )
    tile = found[columns : columns + GROUP]
    msg_x[0:total, :] = square.T[0:total, :]
    msg_x[total : total + GROUP, :] = tile

    x_copies = [
        remote(msg_x, slots_x.at[x], x_send.at[p], x_recv.at[x], cells_device(p * 4 + z_hi)) for p in x_peers
    ]
    for copy in x_copies:
        copy.start()

    head_up.wait_recv()
    head_down.wait_recv()
    half_across = 0.5 * head[0]
    half_along = 0.5 * head[1]
    spread = head[2]
    values = [
        1.0 - 4.0 * spread, spread - half_across, spread + half_across, spread - half_along, spread + half_along
    ]
    for n in range(5):
        natural[n] = values[n]

    def widen(r, carry):
        for n in range(5):
            coef[n, r] = jnp.broadcast_to(natural[n, pl.ds(r, 1), :], (GROUP, width))
        return carry

    lax.fori_loop(1, extent - 1, widen, 0)

    def cov_section(_, fields):
        new = []
        for f in fields:
            new.append(
                values[0] * f
                + values[1] * pltpu.roll(f, extent - 1, 0)
                + values[2] * pltpu.roll(f, 1, 0)
                + values[3] * pltpu.roll(f, width - 1, 1)
                + values[4] * pltpu.roll(f, 1, 1)
            )
        return tuple(new)

    fields = lax.fori_loop(0, SECTIONS, cov_section, (head[3], head[4]))
    span = 2 * grid_rows

    def block_of(position, blocks=1):
        return gathered.at[:, pl.ds(pl.multiple_of(position * span, span), blocks * span), :]

    for u in range(2):
        rows = pl.ds(pl.multiple_of(mine * span + u * grid_rows, grid_rows), grid_rows)
        for v in range(width // LANES):
            gathered[v, rows, :] = fields[u][SECTIONS:top, v * LANES : (v + 1) * LANES]
    pair = core * 8 + y * 2 + (1 - z_lo)
    pair_copy = remote(
        block_of(mine), block_of(mine), pair_send, pair_recv, cols_device((1 - z_lo) * 8 + y * 2 + core)
    )
    pair_copy.start()

    for p, copy in zip(x_peers, x_copies):
        remote(msg_x, slots_x.at[p], x_send.at[p], x_recv.at[p], cells_device(p * 4 + z_hi)).wait_recv()
    summed = msg_x[...]
    for p in x_peers:
        summed = summed + slots_x[p]
    msg_z[...] = summed
    z_copies = [
        remote(msg_z, slots_z.at[z_hi], z_send.at[p], z_recv.at[z_hi], cells_device(x * 4 + p)) for p in z_peers
    ]
    for copy in z_copies:
        copy.start()

    def stencil(g):
        rows = pl.ds(pl.multiple_of(g * GROUP, GROUP), GROUP)

        def read(r, section):
            if section == 0:
                if r < SECTIONS:
                    return low[rows, r * width : (r + 1) * width]
                if r < top:
                    return own[rows, (r - SECTIONS) * width : (r - SECTIONS + 1) * width]
                return high[rows, (r - top) * width : (r - top + 1) * width]
            return (buf_a if section % 2 else buf_b)[r]

        for section in range(SECTIONS):
            first, last = section + 1, extent - section - 1
            below, here = read(first - 1, section), read(first, section)
            for r in range(first, last):
                above = read(r + 1, section)
                new = (
                    coef[0, r] * here
                    + coef[1, r] * above
                    + coef[2, r] * below
                    + coef[3, r] * pltpu.roll(here, width - 1, 1)
                    + coef[4, r] * pltpu.roll(here, 1, 1)
                )
                if section == SECTIONS - 1:
                    result[rows, (r - SECTIONS) * width : (r - SECTIONS + 1) * width] = new
                else:
                    (buf_b if section % 2 else buf_a)[r] = new
                below, here = here, above

    def finish(g):
        rows = pl.ds(pl.multiple_of(g * GROUP, GROUP), GROUP)
        for i in range(grid_rows):
            part = slice(i * width, (i + 1) * width)
            result[rows, part] = result[rows, part] - corr[i, rows, :]
        pltpu.make_async_copy(result.at[rows, :], out_ref.at[rows, :], out_sem.at[g]).start()

    def after_first():
        remote(block_of(pair), block_of(pair), pair_send, pair_recv, cols_device((1 - z_lo) * 8 + y * 2 + core)).wait_recv()
        here = block_of(core * 8 + y * 2, 2)
        for p in y_peers:
            remote(here, here, y_send.at[p], y_recv.at[y], cols_device(z_lo * 8 + p * 2 + core)).start()
        for p in z_peers:
            remote(msg_z, slots_z.at[p], z_send.at[p], z_recv.at[p], cells_device(x * 4 + p)).wait_recv()
        summed = msg_z[...]
        for p in z_peers:
            summed = summed + slots_z[p]
        msg_c[...] = summed
        for p in c_peers:
            remote(
                msg_c.at[total : total + GROUP, :], slots_c.at[c], c_send.at[p], c_recv.at[c], cols_device(p)
            ).start()
        slots_c[c] = summed[total : total + GROUP, :]

    def after_second():
        for p in y_peers:
            there = block_of(core * 8 + p * 2, 2)
            remote(there, there, y_send.at[p], y_recv.at[p], cols_device(z_lo * 8 + p * 2 + core)).wait_recv()
        half = block_of(core * 8, 8)
        remote(half, half, core_send, core_recv, cols_device(z_lo * 8 + y * 2 + (1 - core))).start()
        for p in c_peers:
            remote(
                msg_c.at[total : total + GROUP, :], slots_c.at[p], c_send.at[p], c_recv.at[p], cols_device(p)
            ).wait_recv()
        order = sorted(range(count), key=place)
        quarters = []
        for b in range(4):
            quarter = slots_c[order[4 * b]]
            for n in range(1, 4):
                quarter = quarter + slots_c[order[4 * b + n]]
            quarters.append(quarter)
        entries = jnp.concatenate(quarters, axis=0)
        turned = jnp.concatenate(
            [entries, jnp.zeros((LANES - total, LANES), jnp.float32)], axis=0
        ).T[0:total, :]
        row = lax.broadcasted_iota(jnp.int32, (total, LANES), 0)
        col = lax.broadcasted_iota(jnp.int32, (total, LANES), 1)
        row_u, col_u = jnp.bitwise_and(row, 1), jnp.bitwise_and(col, 1)
        system = jnp.where(
            row_u == col_u, 0.5 * (entries + turned), jnp.where(row_u < col_u, entries, turned)
        )
        noise = jnp.zeros((total, LANES), jnp.float32)
        for u in range(2):
            for k in range(count):
                noise = jnp.where(row == place(k) * 2 + u, noise_ref[u, k], noise)
        system = system + jnp.where(row == col, noise, 0.0)
        system = jnp.where(col < total, system, msg_c[0:total, :])
        for u in range(2):
            for k in range(count):
                q = place(k) * 2 + u
                scaled = system[q : q + 1, :] / system[q : q + 1, q : q + 1]
                system = jnp.where(row == q, scaled, system - system[:, q : q + 1] * scaled)
        weights = jnp.concatenate(
            [system, jnp.zeros((LANES - total, LANES), jnp.float32)], axis=0
        ).T[total : total + columns, :]
        upper = weights.astype(jnp.bfloat16).astype(jnp.float32)
        lower = weights - upper
        weight[...] = (
            upper + pltpu.roll(upper, total, 1) + pltpu.roll(lower, 2 * total, 1) + pltpu.roll(lower, 3 * total, 1)
        )

    def after_third():
        there = block_of((1 - core) * 8, 8)
        remote(there, there, core_send, core_recv, cols_device(z_lo * 8 + y * 2 + (1 - core))).wait_recv()
        left = weight[...].astype(jnp.bfloat16)

        def one_row(i, carry):
            rows = jnp.concatenate(
                [gathered[v, pl.ds(i, total, stride=grid_rows), :] for v in range(width // LANES)], axis=1
            )
            upper = rows.astype(jnp.bfloat16)
            lower = (rows - upper.astype(jnp.float32)).astype(jnp.bfloat16)
            right = jnp.concatenate([upper, lower, upper, lower], axis=0)
            corr[i] = jnp.dot(left, right, preferred_element_type=jnp.float32)
            return carry

        lax.fori_loop(0, grid_rows, one_row, 0)

    def step(g, carry):
        for copy in halos(g):
            copy.wait_recv()

        stencil(g)

        @pl.when(g == 0)
        def _():
            after_first()

        @pl.when(g == 1)
        def _():
            after_second()

        @pl.when(g == 2)
        def _():
            after_third()
            finish(0)
            finish(1)

        @pl.when(g >= 2)
        def _():
            finish(g)

        for copy in halos(g):
            copy.wait_send()

        @pl.when(g + AHEAD < groups)
        def _():
            for copy in halos(g + AHEAD):
                copy.start()

        return carry

    lax.fori_loop(0, groups, step, 0)

    for copy in [head_up, head_down, pair_copy]:
        copy.wait_send()
    for copy in x_copies + z_copies:
        copy.wait_send()
    for p in y_peers:
        here = block_of(core * 8 + y * 2, 2)
        remote(here, here, y_send.at[p], y_recv.at[p], cols_device(z_lo * 8 + p * 2 + core)).wait_send()
    half = block_of(core * 8, 8)
    remote(half, half, core_send, core_recv, cols_device(z_lo * 8 + y * 2 + (1 - core))).wait_send()
    for p in c_peers:
        remote(
            msg_c.at[total : total + GROUP, :], slots_c.at[c], c_send.at[p], c_recv.at[p], cols_device(p)
        ).wait_send()
    for g in range(groups):
        rows = pl.ds(g * GROUP, GROUP)
        pltpu.make_async_copy(result.at[rows, :], out_ref.at[rows, :], out_sem.at[g]).wait()


def local(
    slab_cols, observed_cov, observed_cells, noise_variance, wind_across, wind_along, diffusion
):
    columns, local_cells = slab_cols.shape
    grid_rows, width = wind_across.shape
    count = observed_cells.shape[1]
    total = 2 * count
    extent = grid_rows + 2 * SECTIONS
    edge = SECTIONS * width
    groups = columns // GROUP
    f32 = jnp.float32
    dma = pltpu.SemaphoreType.DMA
    any_space = pl.BlockSpec(memory_space=pltpu.HBM)
    scalars = pl.BlockSpec(memory_space=pltpu.SMEM)
    return pl.pallas_call(
        kernel,
        out_shape=jax.ShapeDtypeStruct((columns, local_cells), f32),
        in_specs=[scalars, scalars] + [any_space] * 5,
        out_specs=pl.BlockSpec(memory_space=pl.ANY),
        scratch_shapes=[
            pltpu.VMEM((columns, local_cells), f32),
            pltpu.VMEM((columns, edge), f32),
            pltpu.VMEM((columns, edge), f32),
            pltpu.VMEM((2, 1, local_cells), f32),
            pltpu.VMEM((5, extent, width), f32),
            pltpu.VMEM((5, extent, width), f32),
            pltpu.VMEM((5, extent, GROUP, width), f32),
            pltpu.VMEM((extent, GROUP, width), f32),
            pltpu.VMEM((extent, GROUP, width), f32),
            pltpu.VMEM((width // LANES, total * grid_rows, LANES), f32),
            pltpu.VMEM((grid_rows, columns, width), f32),
            pltpu.VMEM((columns, local_cells), f32),
            pltpu.VMEM((columns, LANES), f32),
            pltpu.VMEM((total + GROUP, LANES), f32),
            pltpu.VMEM((4, total + GROUP, LANES), f32),
            pltpu.VMEM((total + GROUP, LANES), f32),
            pltpu.VMEM((4, total + GROUP, LANES), f32),
            pltpu.VMEM((total + GROUP, LANES), f32),
            pltpu.VMEM((16, GROUP, LANES), f32),
            dma((5,)),
            dma((groups,)),
            dma((2, groups)),
            dma((2, groups)),
            dma((2,)),
            dma((2,)),
            dma((4,)),
            dma((4,)),
            dma((4,)),
            dma((4,)),
            dma((16,)),
            dma((16,)),
            dma,
            dma,
            dma((4,)),
            dma((4,)),
            dma,
            dma,
        ],
        compiler_params=pltpu.CompilerParams(
            collective_id=0, has_side_effects=True, vmem_limit_bytes=60 * 1024 * 1024
        ),
    )(observed_cells, noise_variance, slab_cols, observed_cov, wind_across, wind_along, diffusion)


def solution(mesh):
    return jax.shard_map(
        local,
        mesh=mesh,
        in_specs=(
            P("cols", "cells"),
            P(None, "cols", "cells"),
            P(),
            P(),
            P("cells", None),
            P("cells", None),
            P("cells", None),
        ),
        out_specs=P("cols", "cells"),
        check_vma=False,
    )
```

```python
import jax
import jax.numpy as jnp
from jax import lax
from jax.experimental import pallas as pl
from jax.experimental.pallas import tpu as pltpu
from jax.sharding import PartitionSpec as P

SECTIONS = 8
GROUP = 8
LANES = 128
AHEAD = 6
STEP_X, STEP_PAIR, STEP_Y, STEP_CORE, STEP_CORR = 0, 3, 6, 9, 11
MESH = pl.DeviceIdType.MESH


def place(k):
    return (k % 2) * 8 + ((k // 2) % 4) * 2 + k // 8


def kernel(
    cells_ref, noise_ref, slab_ref, cov_ref, across_ref, along_ref, spread_ref, result,
    own, low, high, flat, head, natural, coef, buf_a, buf_b, gathered, corr, weight, right_side,
    msg_x, slots_x, msg_z, slots_z, msg_c, slots_c,
    local_sem, halo_send, halo_recv, head_send, head_recv,
    x_send, x_recv, z_send, z_recv, e_send, e_recv,
    pair_send, pair_recv, y_send, y_recv, core_send, core_recv,
):
    columns, local_cells = slab_ref.shape
    grid_rows, width = across_ref.shape
    count = cells_ref.shape[1]
    total = 2 * count
    groups = columns // GROUP
    edge = SECTIONS * width
    extent = grid_rows + 2 * SECTIONS

    c = lax.axis_index("cols")
    t = lax.axis_index("cells")
    core, y, z_lo = lax.rem(c, 2), lax.rem(lax.div(c, 2), 4), lax.div(c, 8)
    x, z_hi = lax.div(t, 4), lax.rem(t, 4)
    mine = core * 8 + y * 2 + z_lo
    after, before = lax.rem(t + 1, 16), lax.rem(t + 15, 16)

    def cells_device(target):
        return {"cells": target}

    def cols_device(target):
        return {"cols": target}

    def remote(src, dst, send, recv, device):
        return pltpu.make_async_remote_copy(
            src_ref=src, dst_ref=dst, send_sem=send, recv_sem=recv, device_id=device, device_id_type=MESH
        )

    x_peers = [lax.rem(x + d, 4) for d in range(1, 4)]
    z_peers = [lax.rem(z_hi + d, 4) for d in range(1, 4)]
    y_peers = [lax.rem(y + d, 4) for d in range(1, 4)]

    locals_ = [
        pltpu.make_async_copy(cov_ref, flat, local_sem.at[0]),
        pltpu.make_async_copy(across_ref, head.at[0, SECTIONS : SECTIONS + grid_rows], local_sem.at[1]),
        pltpu.make_async_copy(along_ref, head.at[1, SECTIONS : SECTIONS + grid_rows], local_sem.at[2]),
        pltpu.make_async_copy(spread_ref, head.at[2, SECTIONS : SECTIONS + grid_rows], local_sem.at[3]),
        pltpu.make_async_copy(slab_ref, own, local_sem.at[4]),
    ]
    for copy in locals_:
        copy.start()

    barrier = pltpu.get_barrier_semaphore()
    peers = (
        [cells_device(after), cells_device(before)]
        + [cells_device(p * 4 + z_hi) for p in x_peers]
        + [cells_device(x * 4 + p) for p in z_peers]
        + [cols_device(z_lo * 8 + p * 2 + core) for p in y_peers]
        + [cols_device(z_lo * 8 + p * 2 + (1 - core)) for p in y_peers]
        + [cols_device((1 - z_lo) * 8 + y * 2 + core), cols_device(z_lo * 8 + y * 2 + (1 - core))]
    )
    for device in peers:
        pl.semaphore_signal(barrier, inc=1, device_id=device, device_id_type=MESH)

    for copy in locals_[:4]:
        copy.wait()
    for u in range(2):
        for i in range(grid_rows):
            head[3 + u, SECTIONS + i : SECTIONS + i + 1, :] = flat[u, :, i * width : (i + 1) * width]
    locals_[4].wait()
    part = 2 * width
    row_q = lax.broadcasted_iota(jnp.int32, (total, LANES), 0)
    wanted = jnp.zeros((total, LANES), jnp.int32)
    for u in range(2):
        for k in range(count):
            wanted = jnp.where(row_q == place(k) * 2 + u, cells_ref[u, k], wanted)
    wanted = jnp.concatenate([wanted] * (part // LANES), axis=1) - t * local_cells
    lane = lax.broadcasted_iota(jnp.int32, (total, part), 1)
    sub_8 = lax.broadcasted_iota(jnp.int32, (GROUP, part), 0)
    first_row = 2 * lax.rem(mine, 4)
    bf16 = jnp.bfloat16

    def pick(n, found):
        start = pl.multiple_of(n * part, part)
        chosen = jnp.where(lane + start == wanted, 1.0, 0.0).astype(bf16)
        rows = jnp.where(
            sub_8 == first_row,
            flat[0, :, pl.ds(start, part)],
            jnp.where(sub_8 == first_row + 1, flat[1, :, pl.ds(start, part)], 0.0),
        )
        block = jnp.concatenate([own[:, pl.ds(start, part)], rows, jnp.zeros_like(rows)], axis=0)
        upper = block.astype(bf16)
        rest = block - upper.astype(jnp.float32)
        middle = rest.astype(bf16)
        lower = (rest - middle.astype(jnp.float32)).astype(bf16)
        pieces = jnp.concatenate([upper, middle, lower], axis=0)
        return found + lax.dot_general(
            pieces, chosen, (((1,), (1,)), ((), ())), preferred_element_type=jnp.float32
        )

    height = columns + 2 * GROUP
    found = lax.fori_loop(
        0, local_cells // part, pick, jnp.zeros((3 * height, total), jnp.float32)
    )
    found = found[0:height] + found[height : 2 * height] + found[2 * height : 3 * height]
    found = jnp.concatenate([found, jnp.zeros((height, LANES - total), jnp.float32)], axis=1)
    square = jnp.concatenate(
        [
            jnp.zeros((total, LANES), jnp.float32),
            found[0:columns],
            jnp.zeros((LANES - total - columns, LANES), jnp.float32),
        ],
        axis=0,
    )
    tile = found[columns : columns + GROUP]
    msg_z[0:total, :] = square.T[0:total, :]
    msg_z[total : total + GROUP, :] = tile

    pl.semaphore_wait(barrier, len(peers))

    top = SECTIONS + grid_rows
    head_up = remote(
        head.at[:, grid_rows : grid_rows + SECTIONS, :], head.at[:, 0:SECTIONS, :],
        head_send.at[0], head_recv.at[0], cells_device(after),
    )
    head_down = remote(
        head.at[:, SECTIONS : 2 * SECTIONS, :], head.at[:, top : top + SECTIONS, :],
        head_send.at[1], head_recv.at[1], cells_device(before),
    )
    z_copies = [
        remote(msg_z, slots_z.at[z_hi], z_send.at[p], z_recv.at[z_hi], cells_device(x * 4 + p)) for p in z_peers
    ]
    for copy in z_copies:
        copy.start()
    head_up.start()
    head_down.start()

    def halos(n):
        rows = pl.ds(pl.multiple_of(lax.div(n, 2) * GROUP, GROUP), GROUP)
        piece = edge // 2
        shift = lax.rem(n, 2) * piece
        here = pl.ds(pl.multiple_of(shift, piece), piece)
        last = pl.ds(pl.multiple_of(local_cells - edge + shift, piece), piece)
        return (
            remote(
                slab_ref.at[rows, last], low.at[rows, here],
                halo_send.at[0, n], halo_recv.at[0, n], cells_device(after),
            ),
            remote(
                slab_ref.at[rows, here], high.at[rows, here],
                halo_send.at[1, n], halo_recv.at[1, n], cells_device(before),
            ),
        )

    for n in range(AHEAD):
        for copy in halos(n):
            copy.start()

    other = core * 8 + y * 2 + (1 - z_lo)
    span = 2 * grid_rows

    def block_of(position, blocks=1):
        return gathered.at[:, pl.ds(pl.multiple_of(position * span, span), blocks * span), :]

    def x_copy(slot, p):
        return remote(msg_x, slots_x.at[slot], x_send.at[p], x_recv.at[slot], cells_device(p * 4 + z_hi))

    def pair_copy(position):
        return remote(
            block_of(position), block_of(position), pair_send.at[0], pair_recv.at[0],
            cols_device((1 - z_lo) * 8 + y * 2 + core),
        )

    def pair_entries(slot):
        return remote(
            msg_c, slots_c.at[slot], pair_send.at[1], pair_recv.at[1],
            cols_device((1 - z_lo) * 8 + y * 2 + core),
        )

    def y_copy(source, p):
        both = block_of(core * 8 + source * 2, 2)
        return remote(both, both, y_send.at[p], y_recv.at[source], cols_device(z_lo * 8 + p * 2 + core))

    def core_copy(source):
        half = block_of(source * 8, 8)
        return remote(half, half, core_send, core_recv, cols_device(z_lo * 8 + y * 2 + (1 - core)))

    others = [(core, p) for p in y_peers] + [(1 - core, p) for p in y_peers] + [(1 - core, y)]

    def entries_copy(source, target):
        mate = source[0] * 4 + source[1]
        two = slots_c.at[pl.ds(mate * 2, 2)]
        return remote(
            two, two, e_send.at[target[0] * 4 + target[1]], e_recv.at[mate],
            cols_device(z_lo * 8 + target[1] * 2 + target[0]),
        )

    def stencil(g):
        rows = pl.ds(pl.multiple_of(g * GROUP, GROUP), GROUP)

        def read(r, section):
            if section == 0:
                if r < SECTIONS:
                    return low[rows, r * width : (r + 1) * width]
                if r < top:
                    return own[rows, (r - SECTIONS) * width : (r - SECTIONS + 1) * width]
                return high[rows, (r - top) * width : (r - top + 1) * width]
            return (buf_a if section % 2 else buf_b)[r]

        for section in range(SECTIONS):
            first, last = section + 1, extent - section - 1
            below, here = read(first - 1, section), read(first, section)
            for r in range(first, last):
                above = read(r + 1, section)
                new = (
                    coef[0, r] * here
                    + coef[1, r] * above
                    + coef[2, r] * below
                    + coef[3, r] * pltpu.roll(here, width - 1, 1)
                    + coef[4, r] * pltpu.roll(here, 1, 1)
                )
                if section == SECTIONS - 1:
                    result[rows, (r - SECTIONS) * width : (r - SECTIONS + 1) * width] = new
                else:
                    (buf_b if section % 2 else buf_a)[r] = new
                below, here = here, above

    def finish(g):
        rows = pl.ds(pl.multiple_of(g * GROUP, GROUP), GROUP)
        for i in range(grid_rows):
            part = slice(i * width, (i + 1) * width)
            result[rows, part] = result[rows, part] - corr[i, rows, :]

    def send_x():
        for p in z_peers:
            remote(msg_z, slots_z.at[p], z_send.at[p], z_recv.at[p], cells_device(x * 4 + p)).wait_recv()
        summed = msg_z[...]
        for p in z_peers:
            summed = summed + slots_z[p]
        msg_x[...] = summed
        for p in x_peers:
            x_copy(x, p).start()

    def forecast_cov():
        head_up.wait_recv()
        head_down.wait_recv()
        half_across = 0.5 * head[0]
        half_along = 0.5 * head[1]
        spread = head[2]
        values = [
            1.0 - 4.0 * spread, spread - half_across, spread + half_across, spread - half_along, spread + half_along
        ]
        for n in range(5):
            natural[n] = values[n]

        def widen(r, carry):
            for n in range(5):
                coef[n, r] = jnp.broadcast_to(natural[n, pl.ds(r, 1), :], (GROUP, width))
            return carry

        lax.fori_loop(1, extent - 1, widen, 0)

        def cov_section(_, fields):
            new = []
            for f in fields:
                new.append(
                    values[0] * f
                    + values[1] * pltpu.roll(f, extent - 1, 0)
                    + values[2] * pltpu.roll(f, 1, 0)
                    + values[3] * pltpu.roll(f, width - 1, 1)
                    + values[4] * pltpu.roll(f, 1, 1)
                )
            return tuple(new)

        fields = lax.fori_loop(0, SECTIONS, cov_section, (head[3], head[4]))
        for u in range(2):
            rows = pl.ds(pl.multiple_of(mine * span + u * grid_rows, grid_rows), grid_rows)
            for v in range(width // LANES):
                gathered[v, rows, :] = fields[u][SECTIONS:top, v * LANES : (v + 1) * LANES]
        pair_copy(mine).start()

    def send_pair():
        for p in x_peers:
            x_copy(p, p).wait_recv()
        summed = msg_x[...]
        for p in x_peers:
            summed = summed + slots_x[p]
        right_side[...] = summed[0:total, :]
        msg_c[...] = summed[total : total + GROUP, :]
        slots_c[mine] = summed[total : total + GROUP, :]
        pair_entries(mine).start()
        pair_copy(other).wait_recv()
        for p in y_peers:
            y_copy(y, p).start()

    def send_entries():
        pair_entries(other).wait_recv()
        for target in others:
            entries_copy((core, y), target).start()

    def send_core():
        for p in y_peers:
            y_copy(p, p).wait_recv()
        core_copy(core).start()

    def solve():
        for source in others:
            entries_copy(source, source).wait_recv()
        quarters = []
        for b in range(4):
            quarter = slots_c[4 * b]
            for n in range(1, 4):
                quarter = quarter + slots_c[4 * b + n]
            quarters.append(quarter)
        entries = jnp.concatenate(quarters, axis=0)
        turned = jnp.concatenate(
            [entries, jnp.zeros((LANES - total, LANES), jnp.float32)], axis=0
        ).T[0:total, :]
        row = lax.broadcasted_iota(jnp.int32, (total, LANES), 0)
        col = lax.broadcasted_iota(jnp.int32, (total, LANES), 1)
        row_u, col_u = jnp.bitwise_and(row, 1), jnp.bitwise_and(col, 1)
        system = jnp.where(
            row_u == col_u, 0.5 * (entries + turned), jnp.where(row_u < col_u, entries, turned)
        )
        noise = jnp.zeros((total, LANES), jnp.float32)
        for u in range(2):
            for k in range(count):
                noise = jnp.where(row == place(k) * 2 + u, noise_ref[u, k], noise)
        system = system + jnp.where(row == col, noise, 0.0)
        system = jnp.where(col < total, system, right_side[...])
        for u in range(2):
            for k in range(count):
                q = place(k) * 2 + u
                scaled = system[q : q + 1, :] / system[q : q + 1, q : q + 1]
                system = jnp.where(row == q, scaled, system - system[:, q : q + 1] * scaled)
        weights = jnp.concatenate(
            [system, jnp.zeros((LANES - total, LANES), jnp.float32)], axis=0
        ).T[total : total + columns, :]
        upper = weights.astype(jnp.bfloat16).astype(jnp.float32)
        lower = weights - upper
        weight[...] = (
            upper + pltpu.roll(upper, total, 1) + pltpu.roll(lower, 2 * total, 1) + pltpu.roll(lower, 3 * total, 1)
        )

    def correct():
        core_copy(1 - core).wait_recv()
        left = weight[...].astype(jnp.bfloat16)

        def one_row(i, carry):
            rows = jnp.concatenate(
                [gathered[v, pl.ds(i, total, stride=grid_rows), :] for v in range(width // LANES)], axis=1
            )
            upper = rows.astype(jnp.bfloat16)
            lower = (rows - upper.astype(jnp.float32)).astype(jnp.bfloat16)
            right = jnp.concatenate([upper, lower, upper, lower], axis=0)
            corr[i] = jnp.dot(left, right, preferred_element_type=jnp.float32)
            return carry

        lax.fori_loop(0, grid_rows, one_row, 0)

    def advance(g):
        for h in range(2):
            for copy in halos(2 * g + h):
                copy.wait_recv()
        stencil(g)

    steps = 2 * groups

    def step(n, carry):
        @pl.when(n < steps)
        def _():
            for copy in halos(n):
                copy.wait_send()

        @pl.when(n + AHEAD < steps)
        def _():
            for copy in halos(n + AHEAD):
                copy.start()

        @pl.when(n == STEP_X)
        def _():
            send_x()
            forecast_cov()

        @pl.when(n == STEP_PAIR)
        def _():
            send_pair()

        @pl.when(n == STEP_Y)
        def _():
            send_entries()

        @pl.when(n == STEP_CORE)
        def _():
            send_core()
            solve()

        @pl.when(n == STEP_CORR)
        def _():
            correct()

        @pl.when(jnp.logical_and(n >= 2, lax.rem(n, 2) == 0))
        def _():
            advance(lax.div(n, 2) - 1)

        @pl.when(jnp.logical_and(n > STEP_CORR, n < steps - 1))
        def _():
            finish(2 * (n - STEP_CORR - 1))
            finish(2 * (n - STEP_CORR - 1) + 1)

        @pl.when(n >= steps - 1)
        def _():
            finish(n - groups - 1)

        return carry

    lax.fori_loop(0, steps + 1, step, 0)

    for copy in [head_up, head_down, pair_copy(mine), pair_entries(mine), core_copy(core)]:
        copy.wait_send()
    for copy in z_copies:
        copy.wait_send()
    for p in x_peers:
        x_copy(x, p).wait_send()
    for p in y_peers:
        y_copy(y, p).wait_send()
    for target in others:
        entries_copy((core, y), target).wait_send()


def local(
    slab_cols, observed_cov, observed_cells, noise_variance, wind_across, wind_along, diffusion
):
    columns, local_cells = slab_cols.shape
    grid_rows, width = wind_across.shape
    count = observed_cells.shape[1]
    total = 2 * count
    extent = grid_rows + 2 * SECTIONS
    edge = SECTIONS * width
    groups = columns // GROUP
    f32 = jnp.float32
    dma = pltpu.SemaphoreType.DMA
    any_space = pl.BlockSpec(memory_space=pltpu.HBM)
    scalars = pl.BlockSpec(memory_space=pltpu.SMEM)
    operands = [
        pltpu.with_memory_space_constraint(a, pltpu.HBM)
        for a in (
            observed_cells, noise_variance, slab_cols, observed_cov, wind_across, wind_along, diffusion
        )
    ]
    return pl.pallas_call(
        kernel,
        out_shape=pltpu.VMEM((columns, local_cells), f32),
        in_specs=[scalars, scalars] + [any_space] * 5,
        out_specs=pl.BlockSpec(memory_space=pltpu.VMEM),
        scratch_shapes=[
            pltpu.VMEM((columns, local_cells), f32),
            pltpu.VMEM((columns, edge), f32),
            pltpu.VMEM((columns, edge), f32),
            pltpu.VMEM((2, 1, local_cells), f32),
            pltpu.VMEM((5, extent, width), f32),
            pltpu.VMEM((5, extent, width), f32),
            pltpu.VMEM((5, extent, GROUP, width), f32),
            pltpu.VMEM((extent, GROUP, width), f32),
            pltpu.VMEM((extent, GROUP, width), f32),
            pltpu.VMEM((width // LANES, total * grid_rows, LANES), f32),
            pltpu.VMEM((grid_rows, columns, width), f32),
            pltpu.VMEM((columns, LANES), f32),
            pltpu.VMEM((total, LANES), f32),
            pltpu.VMEM((total + GROUP, LANES), f32),
            pltpu.VMEM((4, total + GROUP, LANES), f32),
            pltpu.VMEM((total + GROUP, LANES), f32),
            pltpu.VMEM((4, total + GROUP, LANES), f32),
            pltpu.VMEM((GROUP, LANES), f32),
            pltpu.VMEM((16, GROUP, LANES), f32),
            dma((5,)),
            dma((2, 2 * groups)),
            dma((2, 2 * groups)),
            dma((2,)),
            dma((2,)),
            dma((4,)),
            dma((4,)),
            dma((4,)),
            dma((4,)),
            dma((8,)),
            dma((8,)),
            dma((2,)),
            dma((2,)),
            dma((4,)),
            dma((4,)),
            dma,
            dma,
        ],
        compiler_params=pltpu.CompilerParams(
            collective_id=0, has_side_effects=True, vmem_limit_bytes=32 * 1024 * 1024
        ),
    )(*operands)


def solution(mesh):
    return jax.shard_map(
        local,
        mesh=mesh,
        in_specs=(
            P("cols", "cells"),
            P(None, "cols", "cells"),
            P(),
            P(),
            P("cells", None),
            P("cells", None),
            P("cells", None),
        ),
        out_specs=P("cols", "cells"),
        check_vma=False,
    )
```

```python
import jax
import jax.numpy as jnp
from jax import lax
from jax.experimental import pallas as pl
from jax.experimental.pallas import tpu as pltpu
from jax.sharding import PartitionSpec as P

SECTIONS = 8
GROUP = 8
LANES = 128
FIRST = 2
AHEAD = 6
STEP_HEAD, STEP_PAIR, STEP_Y, STEP_CORE, STEP_CORR = 0, 3, 6, 9, 12
MESH = pl.DeviceIdType.MESH


def place(k):
    return (k % 2) * 8 + ((k // 2) % 4) * 2 + k // 8


def kernel(
    cells_ref, noise_ref, slab_ref, cov_ref, across_ref, along_ref, spread_ref, result,
    own, low, high, flat, head, natural, coef, buf_a, buf_b, gathered, corr, weight, right_side,
    msg_x, slots_x, msg_z, slots_z, msg_c, slots_c,
    local_sem, halo_send, halo_recv, head_send, head_recv, wind_send, wind_recv, w_send, w_recv,
    x_send, x_recv, z_send, z_recv, e_send, e_recv,
    pair_send, pair_recv, y_send, y_recv, core_send, core_recv,
):
    columns, local_cells = slab_ref.shape
    grid_rows, width = across_ref.shape
    count = cells_ref.shape[1]
    total = 2 * count
    groups = columns // GROUP
    edge = SECTIONS * width
    extent = grid_rows + 2 * SECTIONS

    c = lax.axis_index("cols")
    t = lax.axis_index("cells")
    core, y, z_lo = lax.rem(c, 2), lax.rem(lax.div(c, 2), 4), lax.div(c, 8)
    x, z_hi = lax.div(t, 4), lax.rem(t, 4)
    mine = core * 8 + y * 2 + z_lo
    after, before = lax.rem(t + 1, 16), lax.rem(t + 15, 16)

    def cells_device(target):
        return {"cells": target}

    def cols_device(target):
        return {"cols": target}

    def remote(src, dst, send, recv, device):
        return pltpu.make_async_remote_copy(
            src_ref=src, dst_ref=dst, send_sem=send, recv_sem=recv, device_id=device, device_id_type=MESH
        )

    x_peers = [lax.rem(x + d, 4) for d in range(1, 4)]
    z_peers = [lax.rem(z_hi + d, 4) for d in range(1, 4)]
    y_peers = [lax.rem(y + d, 4) for d in range(1, 4)]

    locals_ = [
        pltpu.make_async_copy(cov_ref, flat, local_sem.at[0]),
        pltpu.make_async_copy(across_ref, head.at[0, SECTIONS : SECTIONS + grid_rows], local_sem.at[1]),
        pltpu.make_async_copy(along_ref, head.at[1, SECTIONS : SECTIONS + grid_rows], local_sem.at[2]),
        pltpu.make_async_copy(spread_ref, head.at[2, SECTIONS : SECTIONS + grid_rows], local_sem.at[3]),
        pltpu.make_async_copy(slab_ref, own, local_sem.at[4]),
    ]
    for copy in locals_:
        copy.start()

    barrier = pltpu.get_barrier_semaphore()
    peers = (
        [cells_device(after), cells_device(before)]
        + [cells_device(p * 4 + z_hi) for p in x_peers]
        + [cells_device(x * 4 + p) for p in z_peers]
        + [cols_device(z_lo * 8 + p * 2 + core) for p in y_peers]
        + [cols_device(z_lo * 8 + p * 2 + (1 - core)) for p in y_peers]
        + [cols_device((1 - z_lo) * 8 + y * 2 + core), cols_device(z_lo * 8 + y * 2 + (1 - core))]
    )
    for device in peers:
        pl.semaphore_signal(barrier, inc=1, device_id=device, device_id_type=MESH)

    for copy in locals_[:4]:
        copy.wait()
    for u in range(2):
        for i in range(grid_rows):
            head[3 + u, SECTIONS + i : SECTIONS + i + 1, :] = flat[u, :, i * width : (i + 1) * width]
    locals_[4].wait()
    part = 2 * width
    row_q = lax.broadcasted_iota(jnp.int32, (total, LANES), 0)
    wanted = jnp.zeros((total, LANES), jnp.int32)
    for u in range(2):
        for k in range(count):
            wanted = jnp.where(row_q == place(k) * 2 + u, cells_ref[u, k], wanted)
    wanted = jnp.concatenate([wanted] * (part // LANES), axis=1) - t * local_cells
    lane = lax.broadcasted_iota(jnp.int32, (total, part), 1)
    sub_8 = lax.broadcasted_iota(jnp.int32, (GROUP, part), 0)
    first_row = 2 * lax.rem(mine, 4)
    bf16 = jnp.bfloat16

    def pick(n, found):
        start = pl.multiple_of(n * part, part)
        chosen = jnp.where(lane + start == wanted, 1.0, 0.0).astype(bf16)
        rows = jnp.where(
            sub_8 == first_row,
            flat[0, :, pl.ds(start, part)],
            jnp.where(sub_8 == first_row + 1, flat[1, :, pl.ds(start, part)], 0.0),
        )
        block = jnp.concatenate([own[:, pl.ds(start, part)], rows, jnp.zeros_like(rows)], axis=0)
        upper = block.astype(bf16)
        rest = block - upper.astype(jnp.float32)
        middle = rest.astype(bf16)
        lower = (rest - middle.astype(jnp.float32)).astype(bf16)
        pieces = jnp.concatenate([upper, middle, lower], axis=0)
        return found + lax.dot_general(
            pieces, chosen, (((1,), (1,)), ((), ())), preferred_element_type=jnp.float32
        )

    height = columns + 2 * GROUP
    found = lax.fori_loop(
        0, local_cells // part, pick, jnp.zeros((3 * height, total), jnp.float32)
    )
    found = found[0:height] + found[height : 2 * height] + found[2 * height : 3 * height]
    found = jnp.concatenate([found, jnp.zeros((height, LANES - total), jnp.float32)], axis=1)
    rows = columns // 4
    packed = found[0:rows]
    for n in range(1, 4):
        packed = packed + pltpu.roll(found[n * rows : (n + 1) * rows], n * total, 1)
    msg_z[0:rows, :] = packed
    msg_z[rows : rows + GROUP, :] = found[columns : columns + GROUP]
    pl.semaphore_wait(barrier, len(peers))

    top = SECTIONS + grid_rows

    def halos(n):
        rows = pl.ds(pl.multiple_of(lax.div(n, 2) * GROUP, GROUP), GROUP)
        piece = edge // 2
        shift = lax.rem(n, 2) * piece
        here = pl.ds(pl.multiple_of(shift, piece), piece)
        last = pl.ds(pl.multiple_of(local_cells - edge + shift, piece), piece)
        return (
            remote(
                slab_ref.at[rows, last], low.at[rows, here],
                halo_send.at[0, n], halo_recv.at[0, n], cells_device(after),
            ),
            remote(
                slab_ref.at[rows, here], high.at[rows, here],
                halo_send.at[1, n], halo_recv.at[1, n], cells_device(before),
            ),
        )

    quarter = pl.ds(pl.multiple_of(y * LANES, LANES), LANES)
    wind_rows = pl.ds(pl.multiple_of((1 - core) * (grid_rows - SECTIONS), SECTIONS), SECTIONS)
    side = lax.select(core == 0, after, before)
    winds = [
        remote(
            ref.at[wind_rows, quarter], head.at[n, pl.ds(pl.multiple_of(core * top, SECTIONS), SECTIONS), quarter],
            wind_send.at[n], wind_recv.at[n], cells_device(side),
        )
        for n, ref in enumerate((across_ref, along_ref, spread_ref))
    ]
    others = [(core, p) for p in y_peers] + [(1 - core, p) for p in y_peers] + [(1 - core, y)]

    def wind_copy(source, target):
        piece = head.at[
            0:3,
            pl.ds(pl.multiple_of(source[0] * top, SECTIONS), SECTIONS),
            pl.ds(pl.multiple_of(source[1] * LANES, LANES), LANES),
        ]
        return remote(
            piece, piece, w_send.at[target[0] * 4 + target[1]], w_recv.at[source[0] * 4 + source[1]],
            cols_device(z_lo * 8 + target[1] * 2 + target[0]),
        )

    z_copies = [
        remote(msg_z, slots_z.at[z_hi], z_send.at[p], z_recv.at[z_hi], cells_device(x * 4 + p)) for p in z_peers
    ]
    for copy in z_copies:
        copy.start()
    head_up = remote(
        head.at[3:5, grid_rows : grid_rows + SECTIONS, :], head.at[3:5, 0:SECTIONS, :],
        head_send.at[0], head_recv.at[0], cells_device(after),
    )
    head_down = remote(
        head.at[3:5, SECTIONS : 2 * SECTIONS, :], head.at[3:5, top : top + SECTIONS, :],
        head_send.at[1], head_recv.at[1], cells_device(before),
    )
    for copy in winds:
        copy.start()
    head_up.start()
    head_down.start()
    for n in range(FIRST):
        for copy in halos(n):
            copy.start()

    other = core * 8 + y * 2 + (1 - z_lo)
    span = 2 * grid_rows

    def block_of(position, blocks=1):
        return gathered.at[:, pl.ds(pl.multiple_of(position * span, span), blocks * span), :]

    def x_copy(slot, p):
        return remote(msg_x, slots_x.at[slot], x_send.at[p], x_recv.at[slot], cells_device(p * 4 + z_hi))

    def pair_copy(position):
        return remote(
            block_of(position), block_of(position), pair_send.at[0], pair_recv.at[0],
            cols_device((1 - z_lo) * 8 + y * 2 + core),
        )

    def pair_entries(slot):
        return remote(
            msg_c, slots_c.at[slot], pair_send.at[1], pair_recv.at[1],
            cols_device((1 - z_lo) * 8 + y * 2 + core),
        )

    def y_copy(source, p):
        both = block_of(core * 8 + source * 2, 2)
        return remote(both, both, y_send.at[p], y_recv.at[source], cols_device(z_lo * 8 + p * 2 + core))

    def core_copy(source):
        half = block_of(source * 8, 8)
        return remote(half, half, core_send, core_recv, cols_device(z_lo * 8 + y * 2 + (1 - core)))

    def entries_copy(source, target):
        mate = source[0] * 4 + source[1]
        two = slots_c.at[pl.ds(mate * 2, 2)]
        return remote(
            two, two, e_send.at[target[0] * 4 + target[1]], e_recv.at[mate],
            cols_device(z_lo * 8 + target[1] * 2 + target[0]),
        )

    def stencil(g):
        rows = pl.ds(pl.multiple_of(g * GROUP, GROUP), GROUP)

        def read(r, section):
            if section == 0:
                if r < SECTIONS:
                    return low[rows, r * width : (r + 1) * width]
                if r < top:
                    return own[rows, (r - SECTIONS) * width : (r - SECTIONS + 1) * width]
                return high[rows, (r - top) * width : (r - top + 1) * width]
            return (buf_a if section % 2 else buf_b)[r]

        for section in range(SECTIONS):
            first, last = section + 1, extent - section - 1
            below, here = read(first - 1, section), read(first, section)
            for r in range(first, last):
                above = read(r + 1, section)
                new = (
                    coef[0, r] * here
                    + coef[1, r] * above
                    + coef[2, r] * below
                    + coef[3, r] * pltpu.roll(here, width - 1, 1)
                    + coef[4, r] * pltpu.roll(here, 1, 1)
                )
                if section == SECTIONS - 1:
                    result[rows, (r - SECTIONS) * width : (r - SECTIONS + 1) * width] = new
                else:
                    (buf_b if section % 2 else buf_a)[r] = new
                below, here = here, above

    def finish(g):
        rows = pl.ds(pl.multiple_of(g * GROUP, GROUP), GROUP)
        for i in range(grid_rows):
            part = slice(i * width, (i + 1) * width)
            result[rows, part] = result[rows, part] - corr[i, rows, :]

    def send_x():
        for p in z_peers:
            remote(msg_z, slots_z.at[p], z_send.at[p], z_recv.at[p], cells_device(x * 4 + p)).wait_recv()
        summed = msg_z[...]
        for p in z_peers:
            summed = summed + slots_z[p]
        msg_x[...] = summed
        for p in x_peers:
            x_copy(x, p).start()

    def forecast_cov():
        for source in others:
            wind_copy(source, source).wait_recv()
        head_up.wait_recv()
        head_down.wait_recv()
        half_across = 0.5 * head[0]
        half_along = 0.5 * head[1]
        spread = head[2]
        values = [
            1.0 - 4.0 * spread, spread - half_across, spread + half_across, spread - half_along, spread + half_along
        ]
        for n in range(5):
            natural[n] = values[n]

        def widen(r, carry):
            for n in range(5):
                coef[n, r] = jnp.broadcast_to(natural[n, pl.ds(r, 1), :], (GROUP, width))
            return carry

        lax.fori_loop(1, extent - 1, widen, 0)

        def cov_section(_, fields):
            new = []
            for f in fields:
                new.append(
                    values[0] * f
                    + values[1] * pltpu.roll(f, extent - 1, 0)
                    + values[2] * pltpu.roll(f, 1, 0)
                    + values[3] * pltpu.roll(f, width - 1, 1)
                    + values[4] * pltpu.roll(f, 1, 1)
                )
            return tuple(new)

        fields = lax.fori_loop(0, SECTIONS, cov_section, (head[3], head[4]))
        for u in range(2):
            rows = pl.ds(pl.multiple_of(mine * span + u * grid_rows, grid_rows), grid_rows)
            for v in range(width // LANES):
                gathered[v, rows, :] = fields[u][SECTIONS:top, v * LANES : (v + 1) * LANES]
        pair_copy(mine).start()

    def send_pair():
        for p in x_peers:
            x_copy(p, p).wait_recv()
        summed = msg_x[...]
        for p in x_peers:
            summed = summed + slots_x[p]
        quarter_rows = columns // 4
        picks = summed[0:quarter_rows]
        entries = summed[quarter_rows : quarter_rows + GROUP]
        lane = lax.broadcasted_iota(jnp.int32, (quarter_rows, LANES), 1)
        picks = [picks] + [pltpu.roll(picks, LANES - n * total, 1) for n in range(1, 4)]
        square = jnp.concatenate(
            [jnp.zeros((total, LANES), jnp.float32)]
            + [jnp.where(lane < total, block, 0.0) for block in picks]
            + [jnp.zeros((LANES - total - columns, LANES), jnp.float32)],
            axis=0,
        )
        right_side[...] = square.T[0:total, :]
        msg_c[...] = entries
        slots_c[mine] = entries
        pair_entries(mine).start()
        pair_copy(other).wait_recv()
        for p in y_peers:
            y_copy(y, p).start()

    def send_entries():
        pair_entries(other).wait_recv()
        for target in others:
            entries_copy((core, y), target).start()

    def send_core():
        for p in y_peers:
            y_copy(p, p).wait_recv()
        core_copy(core).start()

    def solve():
        for source in others:
            entries_copy(source, source).wait_recv()
        quarters = []
        for b in range(4):
            quarter = slots_c[4 * b]
            for n in range(1, 4):
                quarter = quarter + slots_c[4 * b + n]
            quarters.append(quarter)
        entries = jnp.concatenate(quarters, axis=0)
        turned = jnp.concatenate(
            [entries, jnp.zeros((LANES - total, LANES), jnp.float32)], axis=0
        ).T[0:total, :]
        row = lax.broadcasted_iota(jnp.int32, (total, LANES), 0)
        col = lax.broadcasted_iota(jnp.int32, (total, LANES), 1)
        row_u, col_u = jnp.bitwise_and(row, 1), jnp.bitwise_and(col, 1)
        system = jnp.where(
            row_u == col_u, 0.5 * (entries + turned), jnp.where(row_u < col_u, entries, turned)
        )
        noise = jnp.zeros((total, LANES), jnp.float32)
        for u in range(2):
            for k in range(count):
                noise = jnp.where(row == place(k) * 2 + u, noise_ref[u, k], noise)
        system = system + jnp.where(row == col, noise, 0.0)
        system = jnp.where(col < total, system, right_side[...])
        for u in range(2):
            for k in range(count):
                q = place(k) * 2 + u
                scaled = system[q : q + 1, :] / system[q : q + 1, q : q + 1]
                system = jnp.where(row == q, scaled, system - system[:, q : q + 1] * scaled)
        weights = jnp.concatenate(
            [system, jnp.zeros((LANES - total, LANES), jnp.float32)], axis=0
        ).T[total : total + columns, :]
        upper = weights.astype(jnp.bfloat16).astype(jnp.float32)
        lower = weights - upper
        weight[...] = (
            upper + pltpu.roll(upper, total, 1) + pltpu.roll(lower, 2 * total, 1) + pltpu.roll(lower, 3 * total, 1)
        )

    def correct():
        core_copy(1 - core).wait_recv()
        left = weight[...].astype(jnp.bfloat16)

        def one_row(i, carry):
            rows = jnp.concatenate(
                [gathered[v, pl.ds(i, total, stride=grid_rows), :] for v in range(width // LANES)], axis=1
            )
            upper = rows.astype(jnp.bfloat16)
            lower = (rows - upper.astype(jnp.float32)).astype(jnp.bfloat16)
            right = jnp.concatenate([upper, lower, upper, lower], axis=0)
            corr[i] = jnp.dot(left, right, preferred_element_type=jnp.float32)
            return carry

        lax.fori_loop(0, grid_rows, one_row, 0)

    def advance(g):
        for h in range(2):
            for copy in halos(2 * g + h):
                copy.wait_recv()
        stencil(g)

    steps = 2 * groups

    def step(n, carry):
        @pl.when(n < steps)
        def _():
            for copy in halos(n):
                copy.wait_send()

        @pl.when(n + AHEAD < steps)
        def _():
            for copy in halos(n + AHEAD):
                copy.start()

        @pl.when(n == STEP_HEAD)
        def _():
            forecast_cov()

        @pl.when(n == STEP_PAIR)
        def _():
            send_pair()

        @pl.when(n == STEP_Y)
        def _():
            send_entries()

        @pl.when(n == STEP_CORE)
        def _():
            send_core()
            solve()

        @pl.when(n == STEP_CORR)
        def _():
            correct()

        @pl.when(jnp.logical_and(n >= 2, lax.rem(n, 2) == 0))
        def _():
            advance(lax.div(n, 2) - 1)

        @pl.when(n > STEP_CORR)
        def _():
            finish(2 * (n - STEP_CORR - 1))
            finish(2 * (n - STEP_CORR - 1) + 1)

        return carry

    for copy in winds:
        copy.wait_recv()
    for target in others:
        wind_copy((core, y), target).start()
    send_x()
    for n in range(FIRST, AHEAD):
        for copy in halos(n):
            copy.start()

    lax.fori_loop(0, steps + 1, step, 0)

    for copy in [head_up, head_down, pair_copy(mine), pair_entries(mine), core_copy(core)]:
        copy.wait_send()
    for copy in z_copies + winds:
        copy.wait_send()
    for p in x_peers:
        x_copy(x, p).wait_send()
    for p in y_peers:
        y_copy(y, p).wait_send()
    for target in others:
        entries_copy((core, y), target).wait_send()
        wind_copy((core, y), target).wait_send()


def local(
    slab_cols, observed_cov, observed_cells, noise_variance, wind_across, wind_along, diffusion
):
    columns, local_cells = slab_cols.shape
    grid_rows, width = wind_across.shape
    count = observed_cells.shape[1]
    total = 2 * count
    extent = grid_rows + 2 * SECTIONS
    edge = SECTIONS * width
    groups = columns // GROUP
    f32 = jnp.float32
    dma = pltpu.SemaphoreType.DMA
    any_space = pl.BlockSpec(memory_space=pltpu.HBM)
    scalars = pl.BlockSpec(memory_space=pltpu.SMEM)
    operands = [
        pltpu.with_memory_space_constraint(a, pltpu.HBM)
        for a in (
            observed_cells, noise_variance, slab_cols, observed_cov, wind_across, wind_along, diffusion
        )
    ]
    return pl.pallas_call(
        kernel,
        out_shape=pltpu.VMEM((columns, local_cells), f32),
        in_specs=[scalars, scalars] + [any_space] * 5,
        out_specs=pl.BlockSpec(memory_space=pltpu.VMEM),
        scratch_shapes=[
            pltpu.VMEM((columns, local_cells), f32),
            pltpu.VMEM((columns, edge), f32),
            pltpu.VMEM((columns, edge), f32),
            pltpu.VMEM((2, 1, local_cells), f32),
            pltpu.VMEM((5, extent, width), f32),
            pltpu.VMEM((5, extent, width), f32),
            pltpu.VMEM((5, extent, GROUP, width), f32),
            pltpu.VMEM((extent, GROUP, width), f32),
            pltpu.VMEM((extent, GROUP, width), f32),
            pltpu.VMEM((width // LANES, total * grid_rows, LANES), f32),
            pltpu.VMEM((grid_rows, columns, width), f32),
            pltpu.VMEM((columns, LANES), f32),
            pltpu.VMEM((total, LANES), f32),
            pltpu.VMEM((columns // 4 + GROUP, LANES), f32),
            pltpu.VMEM((4, columns // 4 + GROUP, LANES), f32),
            pltpu.VMEM((columns // 4 + GROUP, LANES), f32),
            pltpu.VMEM((4, columns // 4 + GROUP, LANES), f32),
            pltpu.VMEM((GROUP, LANES), f32),
            pltpu.VMEM((16, GROUP, LANES), f32),
            dma((5,)),
            dma((2, 2 * groups)),
            dma((2, 2 * groups)),
            dma((2,)),
            dma((2,)),
            dma((3,)),
            dma((3,)),
            dma((8,)),
            dma((8,)),
            dma((4,)),
            dma((4,)),
            dma((4,)),
            dma((4,)),
            dma((8,)),
            dma((8,)),
            dma((2,)),
            dma((2,)),
            dma((4,)),
            dma((4,)),
            dma,
            dma,
        ],
        compiler_params=pltpu.CompilerParams(
            collective_id=0, has_side_effects=True, vmem_limit_bytes=32 * 1024 * 1024
        ),
    )(*operands)


def solution(mesh):
    return jax.shard_map(
        local,
        mesh=mesh,
        in_specs=(
            P("cols", "cells"),
            P(None, "cols", "cells"),
            P(),
            P(),
            P("cells", None),
            P("cells", None),
            P("cells", None),
        ),
        out_specs=P("cols", "cells"),
        check_vma=False,
    )
```

```python
import jax
import jax.numpy as jnp
from jax import lax
from jax.experimental import pallas as pl
from jax.experimental.pallas import tpu as pltpu
from jax.sharding import PartitionSpec as P

SECTIONS = 8
GROUP = 8
LANES = 128
FIRST = 2
AHEAD = 3
STEP_HEAD, STEP_PAIR, STEP_Y, STEP_CORE, STEP_CORR = 0, 2, 5, 8, 12
MESH = pl.DeviceIdType.MESH


def place(k):
    return (k % 2) * 8 + ((k // 2) % 4) * 2 + k // 8


def kernel(
    cells_ref, noise_ref, slab_ref, cov_ref, across_ref, along_ref, spread_ref, result,
    own, low, high, flat, head, natural, coef, buf_a, buf_b, gathered, corr, weight, right_side,
    msg_x, slots_x, msg_z, slots_z, msg_c, slots_c,
    local_sem, halo_send, halo_recv, head_send, head_recv, wind_send, wind_recv, w_send, w_recv,
    x_send, x_recv, z_send, z_recv, e_send, e_recv,
    pair_send, pair_recv, y_send, y_recv, core_send, core_recv,
):
    columns, local_cells = slab_ref.shape
    grid_rows, width = across_ref.shape
    count = cells_ref.shape[1]
    total = 2 * count
    groups = columns // GROUP
    edge = SECTIONS * width
    extent = grid_rows + 2 * SECTIONS

    c = lax.axis_index("cols")
    t = lax.axis_index("cells")
    core, y, z_lo = lax.rem(c, 2), lax.rem(lax.div(c, 2), 4), lax.div(c, 8)
    x, z_hi = lax.div(t, 4), lax.rem(t, 4)
    mine = core * 8 + y * 2 + z_lo
    after, before = lax.rem(t + 1, 16), lax.rem(t + 15, 16)

    def cells_device(target):
        return {"cells": target}

    def cols_device(target):
        return {"cols": target}

    def remote(src, dst, send, recv, device):
        return pltpu.make_async_remote_copy(
            src_ref=src, dst_ref=dst, send_sem=send, recv_sem=recv, device_id=device, device_id_type=MESH
        )

    x_peers = [lax.rem(x + d, 4) for d in range(1, 4)]
    z_peers = [lax.rem(z_hi + d, 4) for d in range(1, 4)]
    y_peers = [lax.rem(y + d, 4) for d in range(1, 4)]

    locals_ = [
        pltpu.make_async_copy(cov_ref, flat, local_sem.at[0]),
        pltpu.make_async_copy(across_ref, head.at[0, SECTIONS : SECTIONS + grid_rows], local_sem.at[1]),
        pltpu.make_async_copy(along_ref, head.at[1, SECTIONS : SECTIONS + grid_rows], local_sem.at[2]),
        pltpu.make_async_copy(spread_ref, head.at[2, SECTIONS : SECTIONS + grid_rows], local_sem.at[3]),
        pltpu.make_async_copy(slab_ref, own, local_sem.at[4]),
    ]
    for copy in locals_:
        copy.start()

    barrier = pltpu.get_barrier_semaphore()
    peers = (
        [cells_device(after), cells_device(before)]
        + [cells_device(p * 4 + z_hi) for p in x_peers]
        + [cells_device(x * 4 + p) for p in z_peers]
        + [cols_device(z_lo * 8 + p * 2 + core) for p in y_peers]
        + [cols_device(z_lo * 8 + p * 2 + (1 - core)) for p in y_peers]
        + [cols_device((1 - z_lo) * 8 + y * 2 + core), cols_device(z_lo * 8 + y * 2 + (1 - core))]
    )
    for device in peers:
        pl.semaphore_signal(barrier, inc=1, device_id=device, device_id_type=MESH)

    for copy in locals_[:4]:
        copy.wait()
    for u in range(2):
        for i in range(grid_rows):
            head[3 + u, SECTIONS + i : SECTIONS + i + 1, :] = flat[u, :, i * width : (i + 1) * width]
    locals_[4].wait()
    part = 2 * width
    row_q = lax.broadcasted_iota(jnp.int32, (total, LANES), 0)
    wanted = jnp.zeros((total, LANES), jnp.int32)
    for u in range(2):
        for k in range(count):
            wanted = jnp.where(row_q == place(k) * 2 + u, cells_ref[u, k], wanted)
    wanted = jnp.concatenate([wanted] * (part // LANES), axis=1) - t * local_cells
    lane = lax.broadcasted_iota(jnp.int32, (total, part), 1)
    sub_8 = lax.broadcasted_iota(jnp.int32, (GROUP, part), 0)
    first_row = 2 * lax.rem(mine, 4)
    bf16 = jnp.bfloat16

    def pick(n, found):
        start = pl.multiple_of(n * part, part)
        chosen = jnp.where(lane + start == wanted, 1.0, 0.0).astype(bf16)
        rows = jnp.where(
            sub_8 == first_row,
            flat[0, :, pl.ds(start, part)],
            jnp.where(sub_8 == first_row + 1, flat[1, :, pl.ds(start, part)], 0.0),
        )
        block = jnp.concatenate([own[:, pl.ds(start, part)], rows, jnp.zeros_like(rows)], axis=0)
        upper = block.astype(bf16)
        rest = block - upper.astype(jnp.float32)
        middle = rest.astype(bf16)
        lower = (rest - middle.astype(jnp.float32)).astype(bf16)
        pieces = jnp.concatenate([upper, middle, lower], axis=0)
        return found + lax.dot_general(
            pieces, chosen, (((1,), (1,)), ((), ())), preferred_element_type=jnp.float32
        )

    height = columns + 2 * GROUP
    found = lax.fori_loop(
        0, local_cells // part, pick, jnp.zeros((3 * height, total), jnp.float32)
    )
    found = found[0:height] + found[height : 2 * height] + found[2 * height : 3 * height]
    found = jnp.concatenate([found, jnp.zeros((height, LANES - total), jnp.float32)], axis=1)
    rows = columns // 4
    packed = found[0:rows]
    for n in range(1, 4):
        packed = packed + pltpu.roll(found[n * rows : (n + 1) * rows], n * total, 1)
    msg_z[0:rows, :] = packed
    msg_z[rows : rows + GROUP, :] = found[columns : columns + GROUP]
    pl.semaphore_wait(barrier, len(peers))

    top = SECTIONS + grid_rows

    def halos(n):
        rows = pl.ds(pl.multiple_of(lax.div(n, 2) * GROUP, GROUP), GROUP)
        piece = edge // 2
        far = lax.rem(n, 2)
        above = pl.ds(pl.multiple_of(far * piece, piece), piece)
        below = pl.ds(pl.multiple_of((1 - far) * piece, piece), piece)
        last = pl.ds(pl.multiple_of(local_cells - edge + (1 - far) * piece, piece), piece)
        return (
            remote(
                slab_ref.at[rows, last], low.at[rows, below],
                halo_send.at[0, n], halo_recv.at[0, n], cells_device(after),
            ),
            remote(
                slab_ref.at[rows, above], high.at[rows, above],
                halo_send.at[1, n], halo_recv.at[1, n], cells_device(before),
            ),
        )

    quarter = pl.ds(pl.multiple_of(y * LANES, LANES), LANES)
    wind_rows = pl.ds(pl.multiple_of((1 - core) * (grid_rows - SECTIONS), SECTIONS), SECTIONS)
    side = lax.select(core == 0, after, before)
    winds = [
        remote(
            ref.at[wind_rows, quarter], head.at[n, pl.ds(pl.multiple_of(core * top, SECTIONS), SECTIONS), quarter],
            wind_send.at[n], wind_recv.at[n], cells_device(side),
        )
        for n, ref in enumerate((across_ref, along_ref, spread_ref))
    ]
    others = [(core, p) for p in y_peers] + [(1 - core, p) for p in y_peers] + [(1 - core, y)]

    def wind_copy(source, target):
        piece = head.at[
            0:3,
            pl.ds(pl.multiple_of(source[0] * top, SECTIONS), SECTIONS),
            pl.ds(pl.multiple_of(source[1] * LANES, LANES), LANES),
        ]
        return remote(
            piece, piece, w_send.at[target[0] * 4 + target[1]], w_recv.at[source[0] * 4 + source[1]],
            cols_device(z_lo * 8 + target[1] * 2 + target[0]),
        )

    z_copies = [
        remote(msg_z, slots_z.at[z_hi], z_send.at[p], z_recv.at[z_hi], cells_device(x * 4 + p)) for p in z_peers
    ]
    for copy in z_copies:
        copy.start()
    head_up = remote(
        head.at[3:5, grid_rows : grid_rows + SECTIONS, :], head.at[3:5, 0:SECTIONS, :],
        head_send.at[0], head_recv.at[0], cells_device(after),
    )
    head_down = remote(
        head.at[3:5, SECTIONS : 2 * SECTIONS, :], head.at[3:5, top : top + SECTIONS, :],
        head_send.at[1], head_recv.at[1], cells_device(before),
    )
    for copy in winds:
        copy.start()
    head_up.start()
    head_down.start()
    for n in range(FIRST):
        for copy in halos(n):
            copy.start()

    other = core * 8 + y * 2 + (1 - z_lo)
    span = 2 * grid_rows

    def block_of(position, blocks=1):
        return gathered.at[:, pl.ds(pl.multiple_of(position * span, span), blocks * span), :]

    def x_copy(slot, p):
        return remote(msg_x, slots_x.at[slot], x_send.at[p], x_recv.at[slot], cells_device(p * 4 + z_hi))

    def pair_copy(position):
        return remote(
            block_of(position), block_of(position), pair_send.at[0], pair_recv.at[0],
            cols_device((1 - z_lo) * 8 + y * 2 + core),
        )

    def pair_entries(slot):
        return remote(
            msg_c, slots_c.at[slot], pair_send.at[1], pair_recv.at[1],
            cols_device((1 - z_lo) * 8 + y * 2 + core),
        )

    def y_copy(source, p):
        both = block_of(core * 8 + source * 2, 2)
        return remote(both, both, y_send.at[p], y_recv.at[source], cols_device(z_lo * 8 + p * 2 + core))

    def core_copy(source):
        half = block_of(source * 8, 8)
        return remote(half, half, core_send, core_recv, cols_device(z_lo * 8 + y * 2 + (1 - core)))

    def entries_copy(source, target):
        mate = source[0] * 4 + source[1]
        two = slots_c.at[pl.ds(mate * 2, 2)]
        return remote(
            two, two, e_send.at[target[0] * 4 + target[1]], e_recv.at[mate],
            cols_device(z_lo * 8 + target[1] * 2 + target[0]),
        )

    def stencil(g, ranges):
        rows = pl.ds(pl.multiple_of(g * GROUP, GROUP), GROUP)

        def read(r, section):
            if section == 0:
                if r < SECTIONS:
                    return low[rows, r * width : (r + 1) * width]
                if r < top:
                    return own[rows, (r - SECTIONS) * width : (r - SECTIONS + 1) * width]
                return high[rows, (r - top) * width : (r - top + 1) * width]
            return (buf_a if section % 2 else buf_b)[r]

        for section in range(SECTIONS):
            for first, last in ranges(section):
                below, here = read(first - 1, section), read(first, section)
                for r in range(first, last):
                    above = read(r + 1, section)
                    new = (
                        coef[0, r] * here
                        + coef[1, r] * above
                        + coef[2, r] * below
                        + coef[3, r] * pltpu.roll(here, width - 1, 1)
                        + coef[4, r] * pltpu.roll(here, 1, 1)
                    )
                    if section == SECTIONS - 1:
                        result[rows, (r - SECTIONS) * width : (r - SECTIONS + 1) * width] = new
                    else:
                        (buf_b if section % 2 else buf_a)[r] = new
                    below, here = here, above

    def finish(g):
        rows = pl.ds(pl.multiple_of(g * GROUP, GROUP), GROUP)
        for i in range(grid_rows):
            part = slice(i * width, (i + 1) * width)
            result[rows, part] = result[rows, part] - corr[i, rows, :]

    def send_x():
        for p in z_peers:
            remote(msg_z, slots_z.at[p], z_send.at[p], z_recv.at[p], cells_device(x * 4 + p)).wait_recv()
        summed = msg_z[...]
        for p in z_peers:
            summed = summed + slots_z[p]
        msg_x[...] = summed
        for p in x_peers:
            x_copy(x, p).start()

    def forecast_cov():
        for source in others:
            wind_copy(source, source).wait_recv()
        head_up.wait_recv()
        head_down.wait_recv()
        half_across = 0.5 * head[0]
        half_along = 0.5 * head[1]
        spread = head[2]
        values = [
            1.0 - 4.0 * spread, spread - half_across, spread + half_across, spread - half_along, spread + half_along
        ]
        for n in range(5):
            natural[n] = values[n]

        def widen(r, carry):
            for n in range(5):
                coef[n, r] = jnp.broadcast_to(natural[n, pl.ds(r, 1), :], (GROUP, width))
            return carry

        lax.fori_loop(1, extent - 1, widen, 0)

        def cov_section(_, fields):
            new = []
            for f in fields:
                new.append(
                    values[0] * f
                    + values[1] * pltpu.roll(f, extent - 1, 0)
                    + values[2] * pltpu.roll(f, 1, 0)
                    + values[3] * pltpu.roll(f, width - 1, 1)
                    + values[4] * pltpu.roll(f, 1, 1)
                )
            return tuple(new)

        fields = lax.fori_loop(0, SECTIONS, cov_section, (head[3], head[4]))
        for u in range(2):
            rows = pl.ds(pl.multiple_of(mine * span + u * grid_rows, grid_rows), grid_rows)
            for v in range(width // LANES):
                gathered[v, rows, :] = fields[u][SECTIONS:top, v * LANES : (v + 1) * LANES]
        pair_copy(mine).start()

    def send_pair():
        for p in x_peers:
            x_copy(p, p).wait_recv()
        summed = msg_x[...]
        for p in x_peers:
            summed = summed + slots_x[p]
        quarter_rows = columns // 4
        picks = summed[0:quarter_rows]
        entries = summed[quarter_rows : quarter_rows + GROUP]
        lane = lax.broadcasted_iota(jnp.int32, (quarter_rows, LANES), 1)
        picks = [picks] + [pltpu.roll(picks, LANES - n * total, 1) for n in range(1, 4)]
        square = jnp.concatenate(
            [jnp.zeros((total, LANES), jnp.float32)]
            + [jnp.where(lane < total, block, 0.0) for block in picks]
            + [jnp.zeros((LANES - total - columns, LANES), jnp.float32)],
            axis=0,
        )
        right_side[...] = square.T[0:total, :]
        msg_c[...] = entries
        slots_c[mine] = entries
        pair_entries(mine).start()
        pair_copy(other).wait_recv()
        for p in y_peers:
            y_copy(y, p).start()

    def send_entries():
        pair_entries(other).wait_recv()
        for target in others:
            entries_copy((core, y), target).start()

    def send_core():
        for p in y_peers:
            y_copy(p, p).wait_recv()
        core_copy(core).start()

    def solve():
        for source in others:
            entries_copy(source, source).wait_recv()
        quarters = []
        for b in range(4):
            quarter = slots_c[4 * b]
            for n in range(1, 4):
                quarter = quarter + slots_c[4 * b + n]
            quarters.append(quarter)
        entries = jnp.concatenate(quarters, axis=0)
        turned = jnp.concatenate(
            [entries, jnp.zeros((LANES - total, LANES), jnp.float32)], axis=0
        ).T[0:total, :]
        row = lax.broadcasted_iota(jnp.int32, (total, LANES), 0)
        col = lax.broadcasted_iota(jnp.int32, (total, LANES), 1)
        row_u, col_u = jnp.bitwise_and(row, 1), jnp.bitwise_and(col, 1)
        system = jnp.where(
            row_u == col_u, 0.5 * (entries + turned), jnp.where(row_u < col_u, entries, turned)
        )
        noise = jnp.zeros((total, LANES), jnp.float32)
        for u in range(2):
            for k in range(count):
                noise = jnp.where(row == place(k) * 2 + u, noise_ref[u, k], noise)
        system = system + jnp.where(row == col, noise, 0.0)
        system = jnp.where(col < total, system, right_side[...])
        for u in range(2):
            for k in range(count):
                q = place(k) * 2 + u
                scaled = system[q : q + 1, :] / system[q : q + 1, q : q + 1]
                system = jnp.where(row == q, scaled, system - system[:, q : q + 1] * scaled)
        weights = jnp.concatenate(
            [system, jnp.zeros((LANES - total, LANES), jnp.float32)], axis=0
        ).T[total : total + columns, :]
        upper = weights.astype(jnp.bfloat16).astype(jnp.float32)
        lower = weights - upper
        weight[...] = (
            upper + pltpu.roll(upper, total, 1) + pltpu.roll(lower, 2 * total, 1) + pltpu.roll(lower, 3 * total, 1)
        )

    def correct():
        core_copy(1 - core).wait_recv()
        left = weight[...].astype(jnp.bfloat16)

        def one_row(i, carry):
            rows = jnp.concatenate(
                [gathered[v, pl.ds(i, total, stride=grid_rows), :] for v in range(width // LANES)], axis=1
            )
            upper = rows.astype(jnp.bfloat16)
            lower = (rows - upper.astype(jnp.float32)).astype(jnp.bfloat16)
            right = jnp.concatenate([upper, lower, upper, lower], axis=0)
            corr[i] = jnp.dot(left, right, preferred_element_type=jnp.float32)
            return carry

        lax.fori_loop(0, grid_rows, one_row, 0)

    near = SECTIONS // 2

    def begin(g):
        for copy in halos(2 * g):
            copy.wait_recv()
        stencil(g, lambda s: [(near + s + 1, extent - near - s - 1)])

    def end(g):
        for copy in halos(2 * g + 1):
            copy.wait_recv()
        stencil(g, lambda s: [(s + 1, near + s + 1), (extent - near - s - 1, extent - s - 1)])

    steps = 2 * groups

    def step(n, carry):
        @pl.when(lax.rem(n, 2) == 1)
        def _():
            begin(lax.div(n, 2))

        @pl.when(n < steps)
        def _():
            for copy in halos(n):
                copy.wait_send()

        @pl.when(n + AHEAD < steps)
        def _():
            for copy in halos(n + AHEAD):
                copy.start()

        @pl.when(n == STEP_HEAD)
        def _():
            forecast_cov()

        @pl.when(n == STEP_PAIR)
        def _():
            send_pair()

        @pl.when(n == STEP_Y)
        def _():
            send_entries()

        @pl.when(n == STEP_CORE)
        def _():
            send_core()
            solve()

        @pl.when(n == STEP_CORR)
        def _():
            correct()

        @pl.when(jnp.logical_and(n >= 2, lax.rem(n, 2) == 0))
        def _():
            end(lax.div(n, 2) - 1)

        @pl.when(n > STEP_CORR)
        def _():
            finish(2 * (n - STEP_CORR - 1))
            finish(2 * (n - STEP_CORR - 1) + 1)

        return carry

    for copy in winds:
        copy.wait_recv()
    for target in others:
        wind_copy((core, y), target).start()
    send_x()
    for n in range(FIRST, AHEAD):
        for copy in halos(n):
            copy.start()

    lax.fori_loop(0, steps + 1, step, 0)

    for copy in [head_up, head_down, pair_copy(mine), pair_entries(mine), core_copy(core)]:
        copy.wait_send()
    for copy in z_copies + winds:
        copy.wait_send()
    for p in x_peers:
        x_copy(x, p).wait_send()
    for p in y_peers:
        y_copy(y, p).wait_send()
    for target in others:
        entries_copy((core, y), target).wait_send()
        wind_copy((core, y), target).wait_send()


def local(
    slab_cols, observed_cov, observed_cells, noise_variance, wind_across, wind_along, diffusion
):
    columns, local_cells = slab_cols.shape
    grid_rows, width = wind_across.shape
    count = observed_cells.shape[1]
    total = 2 * count
    extent = grid_rows + 2 * SECTIONS
    edge = SECTIONS * width
    groups = columns // GROUP
    f32 = jnp.float32
    dma = pltpu.SemaphoreType.DMA
    any_space = pl.BlockSpec(memory_space=pltpu.HBM)
    scalars = pl.BlockSpec(memory_space=pltpu.SMEM)
    operands = [
        pltpu.with_memory_space_constraint(a, pltpu.HBM)
        for a in (
            observed_cells, noise_variance, slab_cols, observed_cov, wind_across, wind_along, diffusion
        )
    ]
    return pl.pallas_call(
        kernel,
        out_shape=pltpu.VMEM((columns, local_cells), f32),
        in_specs=[scalars, scalars] + [any_space] * 5,
        out_specs=pl.BlockSpec(memory_space=pltpu.VMEM),
        scratch_shapes=[
            pltpu.VMEM((columns, local_cells), f32),
            pltpu.VMEM((columns, edge), f32),
            pltpu.VMEM((columns, edge), f32),
            pltpu.VMEM((2, 1, local_cells), f32),
            pltpu.VMEM((5, extent, width), f32),
            pltpu.VMEM((5, extent, width), f32),
            pltpu.VMEM((5, extent, GROUP, width), f32),
            pltpu.VMEM((extent, GROUP, width), f32),
            pltpu.VMEM((extent, GROUP, width), f32),
            pltpu.VMEM((width // LANES, total * grid_rows, LANES), f32),
            pltpu.VMEM((grid_rows, columns, width), f32),
            pltpu.VMEM((columns, LANES), f32),
            pltpu.VMEM((total, LANES), f32),
            pltpu.VMEM((columns // 4 + GROUP, LANES), f32),
            pltpu.VMEM((4, columns // 4 + GROUP, LANES), f32),
            pltpu.VMEM((columns // 4 + GROUP, LANES), f32),
            pltpu.VMEM((4, columns // 4 + GROUP, LANES), f32),
            pltpu.VMEM((GROUP, LANES), f32),
            pltpu.VMEM((16, GROUP, LANES), f32),
            dma((5,)),
            dma((2, 2 * groups)),
            dma((2, 2 * groups)),
            dma((2,)),
            dma((2,)),
            dma((3,)),
            dma((3,)),
            dma((8,)),
            dma((8,)),
            dma((4,)),
            dma((4,)),
            dma((4,)),
            dma((4,)),
            dma((8,)),
            dma((8,)),
            dma((2,)),
            dma((2,)),
            dma((4,)),
            dma((4,)),
            dma,
            dma,
        ],
        compiler_params=pltpu.CompilerParams(
            collective_id=0, has_side_effects=True, vmem_limit_bytes=32 * 1024 * 1024
        ),
    )(*operands)


def solution(mesh):
    return jax.shard_map(
        local,
        mesh=mesh,
        in_specs=(
            P("cols", "cells"),
            P(None, "cols", "cells"),
            P(),
            P(),
            P("cells", None),
            P("cells", None),
            P("cells", None),
        ),
        out_specs=P("cols", "cells"),
        check_vma=False,
    )
```

```python
import jax
import jax.numpy as jnp
from jax import lax
from jax.experimental import pallas as pl
from jax.experimental.pallas import tpu as pltpu
from jax.sharding import PartitionSpec as P

SECTIONS = 8
GROUP = 8
LANES = 128
FIRST = 2
AHEAD = 3
STEP_HEAD, STEP_PAIR, STEP_Y, STEP_CORE, STEP_CORR, STEP_END = 0, 2, 5, 8, 10, 12
MESH = pl.DeviceIdType.MESH


def place(k):
    return (k % 2) * 8 + ((k // 2) % 4) * 2 + k // 8


def kernel(
    cells_ref, noise_ref, slab_ref, cov_ref, across_ref, along_ref, spread_ref, result,
    own, low, high, flat, head, natural, coef, buf_a, buf_b, gathered, corr, weight, right_side,
    msg_x, slots_x, msg_z, slots_z, msg_c, slots_c,
    local_sem, halo_send, halo_recv, head_send, head_recv, wind_send, wind_recv, w_send, w_recv,
    x_send, x_recv, z_send, z_recv, e_send, e_recv,
    pair_send, pair_recv, y_send, y_recv, core_send, core_recv,
):
    columns, local_cells = slab_ref.shape
    grid_rows, width = across_ref.shape
    count = cells_ref.shape[1]
    total = 2 * count
    groups = columns // GROUP
    edge = SECTIONS * width
    extent = grid_rows + 2 * SECTIONS

    c = lax.axis_index("cols")
    t = lax.axis_index("cells")
    core, y, z_lo = lax.rem(c, 2), lax.rem(lax.div(c, 2), 4), lax.div(c, 8)
    x, z_hi = lax.div(t, 4), lax.rem(t, 4)
    mine = core * 8 + y * 2 + z_lo
    after, before = lax.rem(t + 1, 16), lax.rem(t + 15, 16)

    def cells_device(target):
        return {"cells": target}

    def cols_device(target):
        return {"cols": target}

    def remote(src, dst, send, recv, device):
        return pltpu.make_async_remote_copy(
            src_ref=src, dst_ref=dst, send_sem=send, recv_sem=recv, device_id=device, device_id_type=MESH
        )

    x_peers = [lax.rem(x + d, 4) for d in range(1, 4)]
    z_peers = [lax.rem(z_hi + d, 4) for d in range(1, 4)]
    y_peers = [lax.rem(y + d, 4) for d in range(1, 4)]

    locals_ = [
        pltpu.make_async_copy(cov_ref, flat, local_sem.at[0]),
        pltpu.make_async_copy(across_ref, head.at[0, SECTIONS : SECTIONS + grid_rows], local_sem.at[1]),
        pltpu.make_async_copy(along_ref, head.at[1, SECTIONS : SECTIONS + grid_rows], local_sem.at[2]),
        pltpu.make_async_copy(spread_ref, head.at[2, SECTIONS : SECTIONS + grid_rows], local_sem.at[3]),
        pltpu.make_async_copy(slab_ref, own, local_sem.at[4]),
    ]
    for copy in locals_:
        copy.start()

    barrier = pltpu.get_barrier_semaphore()
    peers = (
        [cells_device(after), cells_device(before)]
        + [cells_device(p * 4 + z_hi) for p in x_peers]
        + [cells_device(x * 4 + p) for p in z_peers]
        + [cols_device(z_lo * 8 + p * 2 + core) for p in y_peers]
        + [cols_device(z_lo * 8 + p * 2 + (1 - core)) for p in y_peers]
        + [cols_device((1 - z_lo) * 8 + y * 2 + core), cols_device(z_lo * 8 + y * 2 + (1 - core))]
    )
    for device in peers:
        pl.semaphore_signal(barrier, inc=1, device_id=device, device_id_type=MESH)

    for copy in locals_[:4]:
        copy.wait()
    for u in range(2):
        for i in range(grid_rows):
            head[3 + u, SECTIONS + i : SECTIONS + i + 1, :] = flat[u, :, i * width : (i + 1) * width]
    locals_[4].wait()
    part = 2 * width
    row_q = lax.broadcasted_iota(jnp.int32, (total, LANES), 0)
    wanted = jnp.zeros((total, LANES), jnp.int32)
    for u in range(2):
        for k in range(count):
            wanted = jnp.where(row_q == place(k) * 2 + u, cells_ref[u, k], wanted)
    wanted = jnp.concatenate([wanted] * (part // LANES), axis=1) - t * local_cells
    lane = lax.broadcasted_iota(jnp.int32, (total, part), 1)
    sub_8 = lax.broadcasted_iota(jnp.int32, (GROUP, part), 0)
    first_row = 2 * lax.rem(mine, 4)
    bf16 = jnp.bfloat16

    def pick(n, found):
        start = pl.multiple_of(n * part, part)
        chosen = jnp.where(lane + start == wanted, 1.0, 0.0).astype(bf16)
        rows = jnp.where(
            sub_8 == first_row,
            flat[0, :, pl.ds(start, part)],
            jnp.where(sub_8 == first_row + 1, flat[1, :, pl.ds(start, part)], 0.0),
        )
        block = jnp.concatenate([own[:, pl.ds(start, part)], rows, jnp.zeros_like(rows)], axis=0)
        upper = block.astype(bf16)
        rest = block - upper.astype(jnp.float32)
        middle = rest.astype(bf16)
        lower = (rest - middle.astype(jnp.float32)).astype(bf16)
        pieces = jnp.concatenate([upper, middle, lower], axis=0)
        return found + lax.dot_general(
            pieces, chosen, (((1,), (1,)), ((), ())), preferred_element_type=jnp.float32
        )

    height = columns + 2 * GROUP
    found = lax.fori_loop(
        0, local_cells // part, pick, jnp.zeros((3 * height, total), jnp.float32)
    )
    found = found[0:height] + found[height : 2 * height] + found[2 * height : 3 * height]
    found = jnp.concatenate([found, jnp.zeros((height, LANES - total), jnp.float32)], axis=1)
    rows = columns // 4
    packed = found[0:rows]
    for n in range(1, 4):
        packed = packed + pltpu.roll(found[n * rows : (n + 1) * rows], n * total, 1)
    msg_z[0:rows, :] = packed
    msg_z[rows : rows + GROUP, :] = found[columns : columns + GROUP]
    pl.semaphore_wait(barrier, len(peers))

    top = SECTIONS + grid_rows

    def halos(n):
        rows = pl.ds(pl.multiple_of(lax.div(n, 2) * GROUP, GROUP), GROUP)
        piece = edge // 2
        far = lax.rem(n, 2)
        above = pl.ds(pl.multiple_of(far * piece, piece), piece)
        below = pl.ds(pl.multiple_of((1 - far) * piece, piece), piece)
        last = pl.ds(pl.multiple_of(local_cells - edge + (1 - far) * piece, piece), piece)
        return (
            remote(
                slab_ref.at[rows, last], low.at[rows, below],
                halo_send.at[0, n], halo_recv.at[0, n], cells_device(after),
            ),
            remote(
                slab_ref.at[rows, above], high.at[rows, above],
                halo_send.at[1, n], halo_recv.at[1, n], cells_device(before),
            ),
        )

    quarter = pl.ds(pl.multiple_of(y * LANES, LANES), LANES)
    wind_rows = pl.ds(pl.multiple_of((1 - core) * (grid_rows - SECTIONS), SECTIONS), SECTIONS)
    side = lax.select(core == 0, after, before)
    winds = [
        remote(
            ref.at[wind_rows, quarter], head.at[n, pl.ds(pl.multiple_of(core * top, SECTIONS), SECTIONS), quarter],
            wind_send.at[n], wind_recv.at[n], cells_device(side),
        )
        for n, ref in enumerate((across_ref, along_ref, spread_ref))
    ]
    others = [(core, p) for p in y_peers] + [(1 - core, p) for p in y_peers] + [(1 - core, y)]

    def wind_copy(source, target):
        piece = head.at[
            0:3,
            pl.ds(pl.multiple_of(source[0] * top, SECTIONS), SECTIONS),
            pl.ds(pl.multiple_of(source[1] * LANES, LANES), LANES),
        ]
        return remote(
            piece, piece, w_send.at[target[0] * 4 + target[1]], w_recv.at[source[0] * 4 + source[1]],
            cols_device(z_lo * 8 + target[1] * 2 + target[0]),
        )

    z_copies = [
        remote(msg_z, slots_z.at[z_hi], z_send.at[p], z_recv.at[z_hi], cells_device(x * 4 + p)) for p in z_peers
    ]
    for copy in z_copies:
        copy.start()
    head_up = remote(
        head.at[3:5, grid_rows : grid_rows + SECTIONS, :], head.at[3:5, 0:SECTIONS, :],
        head_send.at[0], head_recv.at[0], cells_device(after),
    )
    head_down = remote(
        head.at[3:5, SECTIONS : 2 * SECTIONS, :], head.at[3:5, top : top + SECTIONS, :],
        head_send.at[1], head_recv.at[1], cells_device(before),
    )
    for copy in winds:
        copy.start()
    head_up.start()
    head_down.start()
    for n in range(FIRST):
        for copy in halos(n):
            copy.start()

    other = core * 8 + y * 2 + (1 - z_lo)
    span = 2 * grid_rows

    def block_of(position, blocks=1):
        return gathered.at[:, pl.ds(pl.multiple_of(position * span, span), blocks * span), :]

    def x_copy(slot, p):
        return remote(msg_x, slots_x.at[slot], x_send.at[p], x_recv.at[slot], cells_device(p * 4 + z_hi))

    def pair_copy(position):
        return remote(
            block_of(position), block_of(position), pair_send.at[0], pair_recv.at[0],
            cols_device((1 - z_lo) * 8 + y * 2 + core),
        )

    def pair_entries(slot):
        return remote(
            msg_c, slots_c.at[slot], pair_send.at[1], pair_recv.at[1],
            cols_device((1 - z_lo) * 8 + y * 2 + core),
        )

    def y_copy(source, p):
        both = block_of(core * 8 + source * 2, 2)
        return remote(both, both, y_send.at[p], y_recv.at[source], cols_device(z_lo * 8 + p * 2 + core))

    def core_copy(source):
        half = block_of(source * 8, 8)
        return remote(half, half, core_send, core_recv, cols_device(z_lo * 8 + y * 2 + (1 - core)))

    def entries_copy(source, target):
        mate = source[0] * 4 + source[1]
        two = slots_c.at[pl.ds(mate * 2, 2)]
        return remote(
            two, two, e_send.at[target[0] * 4 + target[1]], e_recv.at[mate],
            cols_device(z_lo * 8 + target[1] * 2 + target[0]),
        )

    def stencil(g, ranges):
        rows = pl.ds(pl.multiple_of(g * GROUP, GROUP), GROUP)

        def read(r, section):
            if section == 0:
                if r < SECTIONS:
                    return low[rows, r * width : (r + 1) * width]
                if r < top:
                    return own[rows, (r - SECTIONS) * width : (r - SECTIONS + 1) * width]
                return high[rows, (r - top) * width : (r - top + 1) * width]
            return (buf_a if section % 2 else buf_b)[r]

        for section in range(SECTIONS):
            for first, last in ranges(section):
                below, here = read(first - 1, section), read(first, section)
                for r in range(first, last):
                    above = read(r + 1, section)
                    new = (
                        coef[0, r] * here
                        + coef[1, r] * above
                        + coef[2, r] * below
                        + coef[3, r] * pltpu.roll(here, width - 1, 1)
                        + coef[4, r] * pltpu.roll(here, 1, 1)
                    )
                    if section == SECTIONS - 1:
                        result[rows, (r - SECTIONS) * width : (r - SECTIONS + 1) * width] = new
                    else:
                        (buf_b if section % 2 else buf_a)[r] = new
                    below, here = here, above

    def finish(g):
        rows = pl.ds(pl.multiple_of(g * GROUP, GROUP), GROUP)
        for i in range(grid_rows):
            part = slice(i * width, (i + 1) * width)
            result[rows, part] = result[rows, part] - corr[i, rows, :]

    def send_x():
        for p in z_peers:
            remote(msg_z, slots_z.at[p], z_send.at[p], z_recv.at[p], cells_device(x * 4 + p)).wait_recv()
        summed = msg_z[...]
        for p in z_peers:
            summed = summed + slots_z[p]
        msg_x[...] = summed
        for p in x_peers:
            x_copy(x, p).start()

    def forecast_cov():
        for source in others:
            wind_copy(source, source).wait_recv()
        head_up.wait_recv()
        head_down.wait_recv()
        half_across = 0.5 * head[0]
        half_along = 0.5 * head[1]
        spread = head[2]
        values = [
            1.0 - 4.0 * spread, spread - half_across, spread + half_across, spread - half_along, spread + half_along
        ]
        for n in range(5):
            natural[n] = values[n]

        def widen(r, carry):
            for n in range(5):
                coef[n, r] = jnp.broadcast_to(natural[n, pl.ds(r, 1), :], (GROUP, width))
            return carry

        lax.fori_loop(1, extent - 1, widen, 0)

        def cov_section(_, fields):
            new = []
            for f in fields:
                new.append(
                    values[0] * f
                    + values[1] * pltpu.roll(f, extent - 1, 0)
                    + values[2] * pltpu.roll(f, 1, 0)
                    + values[3] * pltpu.roll(f, width - 1, 1)
                    + values[4] * pltpu.roll(f, 1, 1)
                )
            return tuple(new)

        fields = lax.fori_loop(0, SECTIONS, cov_section, (head[3], head[4]))
        for u in range(2):
            rows = pl.ds(pl.multiple_of(mine * span + u * grid_rows, grid_rows), grid_rows)
            for v in range(width // LANES):
                gathered[v, rows, :] = fields[u][SECTIONS:top, v * LANES : (v + 1) * LANES]
        pair_copy(mine).start()

    def send_pair():
        for p in x_peers:
            x_copy(p, p).wait_recv()
        summed = msg_x[...]
        for p in x_peers:
            summed = summed + slots_x[p]
        quarter_rows = columns // 4
        picks = summed[0:quarter_rows]
        entries = summed[quarter_rows : quarter_rows + GROUP]
        lane = lax.broadcasted_iota(jnp.int32, (quarter_rows, LANES), 1)
        picks = [picks] + [pltpu.roll(picks, LANES - n * total, 1) for n in range(1, 4)]
        square = jnp.concatenate(
            [jnp.zeros((total, LANES), jnp.float32)]
            + [jnp.where(lane < total, block, 0.0) for block in picks]
            + [jnp.zeros((LANES - total - columns, LANES), jnp.float32)],
            axis=0,
        )
        right_side[...] = square.T[0:total, :]
        msg_c[...] = entries
        slots_c[mine] = entries
        pair_entries(mine).start()
        pair_copy(other).wait_recv()
        for p in y_peers:
            y_copy(y, p).start()

    def send_entries():
        pair_entries(other).wait_recv()
        for target in others:
            entries_copy((core, y), target).start()

    def send_core():
        for p in y_peers:
            y_copy(p, p).wait_recv()
        core_copy(core).start()

    def solve():
        for source in others:
            entries_copy(source, source).wait_recv()
        quarters = []
        for b in range(4):
            quarter = slots_c[4 * b]
            for n in range(1, 4):
                quarter = quarter + slots_c[4 * b + n]
            quarters.append(quarter)
        entries = jnp.concatenate(quarters, axis=0)
        turned = jnp.concatenate(
            [entries, jnp.zeros((LANES - total, LANES), jnp.float32)], axis=0
        ).T[0:total, :]
        row = lax.broadcasted_iota(jnp.int32, (total, LANES), 0)
        col = lax.broadcasted_iota(jnp.int32, (total, LANES), 1)
        row_u, col_u = jnp.bitwise_and(row, 1), jnp.bitwise_and(col, 1)
        system = jnp.where(
            row_u == col_u, 0.5 * (entries + turned), jnp.where(row_u < col_u, entries, turned)
        )
        noise = jnp.zeros((total, LANES), jnp.float32)
        for u in range(2):
            for k in range(count):
                noise = jnp.where(row == place(k) * 2 + u, noise_ref[u, k], noise)
        system = system + jnp.where(row == col, noise, 0.0)
        system = jnp.where(col < total, system, right_side[...])
        for u in range(2):
            for k in range(count):
                q = place(k) * 2 + u
                scaled = system[q : q + 1, :] / system[q : q + 1, q : q + 1]
                system = jnp.where(row == q, scaled, system - system[:, q : q + 1] * scaled)
        weights = jnp.concatenate(
            [system, jnp.zeros((LANES - total, LANES), jnp.float32)], axis=0
        ).T[total : total + columns, :]
        upper = weights.astype(jnp.bfloat16).astype(jnp.float32)
        lower = weights - upper
        weight[...] = (
            upper + pltpu.roll(upper, total, 1) + pltpu.roll(lower, 2 * total, 1) + pltpu.roll(lower, 3 * total, 1)
        )

    def correct():
        core_copy(1 - core).wait_recv()
        left = weight[...].astype(jnp.bfloat16)

        def one_row(i, carry):
            rows = jnp.concatenate(
                [gathered[v, pl.ds(i, total, stride=grid_rows), :] for v in range(width // LANES)], axis=1
            )
            upper = rows.astype(jnp.bfloat16)
            lower = (rows - upper.astype(jnp.float32)).astype(jnp.bfloat16)
            right = jnp.concatenate([upper, lower, upper, lower], axis=0)
            corr[i] = jnp.dot(left, right, preferred_element_type=jnp.float32)
            return carry

        lax.fori_loop(0, grid_rows, one_row, 0)

    near = SECTIONS // 2

    def begin(g):
        for copy in halos(2 * g):
            copy.wait_recv()
        stencil(g, lambda s: [(near + s + 1, extent - near - s - 1)])

    def end(g):
        for copy in halos(2 * g + 1):
            copy.wait_recv()
        stencil(g, lambda s: [(s + 1, near + s + 1), (extent - near - s - 1, extent - s - 1)])

    steps = 2 * groups

    def step(n, carry):
        @pl.when(lax.rem(n, 2) == 1)
        def _():
            begin(lax.div(n, 2))

        @pl.when(n < steps)
        def _():
            for copy in halos(n):
                copy.wait_send()

        @pl.when(n + AHEAD < steps)
        def _():
            for copy in halos(n + AHEAD):
                copy.start()

        @pl.when(n == STEP_HEAD)
        def _():
            forecast_cov()

        @pl.when(n == STEP_PAIR)
        def _():
            send_pair()

        @pl.when(n == STEP_Y)
        def _():
            send_entries()

        @pl.when(n == STEP_CORE)
        def _():
            send_core()
            solve()

        @pl.when(n == STEP_CORR)
        def _():
            correct()

        @pl.when(jnp.logical_and(n >= 2, lax.rem(n, 2) == 0))
        def _():
            end(lax.div(n, 2) - 1)

        @pl.when(n > STEP_END)
        def _():
            finish(2 * (n - STEP_END - 1))
            finish(2 * (n - STEP_END - 1) + 1)

        return carry

    for copy in winds:
        copy.wait_recv()
    for target in others:
        wind_copy((core, y), target).start()
    send_x()
    for n in range(FIRST, AHEAD):
        for copy in halos(n):
            copy.start()

    lax.fori_loop(0, steps + 1, step, 0)

    for copy in [head_up, head_down, pair_copy(mine), pair_entries(mine), core_copy(core)]:
        copy.wait_send()
    for copy in z_copies + winds:
        copy.wait_send()
    for p in x_peers:
        x_copy(x, p).wait_send()
    for p in y_peers:
        y_copy(y, p).wait_send()
    for target in others:
        entries_copy((core, y), target).wait_send()
        wind_copy((core, y), target).wait_send()


def local(
    slab_cols, observed_cov, observed_cells, noise_variance, wind_across, wind_along, diffusion
):
    columns, local_cells = slab_cols.shape
    grid_rows, width = wind_across.shape
    count = observed_cells.shape[1]
    total = 2 * count
    extent = grid_rows + 2 * SECTIONS
    edge = SECTIONS * width
    groups = columns // GROUP
    f32 = jnp.float32
    dma = pltpu.SemaphoreType.DMA
    any_space = pl.BlockSpec(memory_space=pltpu.HBM)
    scalars = pl.BlockSpec(memory_space=pltpu.SMEM)
    operands = [
        pltpu.with_memory_space_constraint(a, pltpu.HBM)
        for a in (
            observed_cells, noise_variance, slab_cols, observed_cov, wind_across, wind_along, diffusion
        )
    ]
    return pl.pallas_call(
        kernel,
        out_shape=pltpu.VMEM((columns, local_cells), f32),
        in_specs=[scalars, scalars] + [any_space] * 5,
        out_specs=pl.BlockSpec(memory_space=pltpu.VMEM),
        scratch_shapes=[
            pltpu.VMEM((columns, local_cells), f32),
            pltpu.VMEM((columns, edge), f32),
            pltpu.VMEM((columns, edge), f32),
            pltpu.VMEM((2, 1, local_cells), f32),
            pltpu.VMEM((5, extent, width), f32),
            pltpu.VMEM((5, extent, width), f32),
            pltpu.VMEM((5, extent, GROUP, width), f32),
            pltpu.VMEM((extent, GROUP, width), f32),
            pltpu.VMEM((extent, GROUP, width), f32),
            pltpu.VMEM((width // LANES, total * grid_rows, LANES), f32),
            pltpu.VMEM((grid_rows, columns, width), f32),
            pltpu.VMEM((columns, LANES), f32),
            pltpu.VMEM((total, LANES), f32),
            pltpu.VMEM((columns // 4 + GROUP, LANES), f32),
            pltpu.VMEM((4, columns // 4 + GROUP, LANES), f32),
            pltpu.VMEM((columns // 4 + GROUP, LANES), f32),
            pltpu.VMEM((4, columns // 4 + GROUP, LANES), f32),
            pltpu.VMEM((GROUP, LANES), f32),
            pltpu.VMEM((16, GROUP, LANES), f32),
            dma((5,)),
            dma((2, 2 * groups)),
            dma((2, 2 * groups)),
            dma((2,)),
            dma((2,)),
            dma((3,)),
            dma((3,)),
            dma((8,)),
            dma((8,)),
            dma((4,)),
            dma((4,)),
            dma((4,)),
            dma((4,)),
            dma((8,)),
            dma((8,)),
            dma((2,)),
            dma((2,)),
            dma((4,)),
            dma((4,)),
            dma,
            dma,
        ],
        compiler_params=pltpu.CompilerParams(
            collective_id=0, has_side_effects=True, vmem_limit_bytes=32 * 1024 * 1024
        ),
    )(*operands)


def solution(mesh):
    return jax.shard_map(
        local,
        mesh=mesh,
        in_specs=(
            P("cols", "cells"),
            P(None, "cols", "cells"),
            P(),
            P(),
            P("cells", None),
            P("cells", None),
            P("cells", None),
        ),
        out_specs=P("cols", "cells"),
        check_vma=False,
    )
```

```python
import jax
import jax.numpy as jnp
from jax import lax
from jax.experimental import pallas as pl
from jax.experimental.pallas import tpu as pltpu
from jax.sharding import PartitionSpec as P

SECTIONS = 8
GROUP = 8
LANES = 128
FIRST = 3
AHEAD = 3
STEP_HEAD, STEP_PAIR, STEP_Y, STEP_CORE, STEP_CORR, STEP_END = 0, 2, 5, 8, 10, 12
MESH = pl.DeviceIdType.MESH


def place(k):
    return (k % 2) * 8 + ((k // 2) % 4) * 2 + k // 8


def kernel(
    cells_ref, noise_ref, slab_ref, cov_ref, across_ref, along_ref, spread_ref, result,
    own, low, high, flat, head, natural, coef, buf_a, buf_b, gathered, corr, weight, right_side,
    msg_x, slots_x, msg_z, slots_z, msg_c, slots_c,
    local_sem, halo_send, halo_recv, head_send, head_recv, wind_send, wind_recv, w_send, w_recv,
    x_send, x_recv, z_send, z_recv, e_send, e_recv,
    pair_send, pair_recv, y_send, y_recv, core_send, core_recv,
):
    columns, local_cells = slab_ref.shape
    grid_rows, width = across_ref.shape
    count = cells_ref.shape[1]
    total = 2 * count
    groups = columns // GROUP
    edge = SECTIONS * width
    extent = grid_rows + 2 * SECTIONS

    c = lax.axis_index("cols")
    t = lax.axis_index("cells")
    core, y, z_lo = lax.rem(c, 2), lax.rem(lax.div(c, 2), 4), lax.div(c, 8)
    x, z_hi = lax.div(t, 4), lax.rem(t, 4)
    mine = core * 8 + y * 2 + z_lo
    after, before = lax.rem(t + 1, 16), lax.rem(t + 15, 16)

    def cells_device(target):
        return {"cells": target}

    def cols_device(target):
        return {"cols": target}

    def remote(src, dst, send, recv, device):
        return pltpu.make_async_remote_copy(
            src_ref=src, dst_ref=dst, send_sem=send, recv_sem=recv, device_id=device, device_id_type=MESH
        )

    x_peers = [lax.rem(x + d, 4) for d in range(1, 4)]
    z_peers = [lax.rem(z_hi + d, 4) for d in range(1, 4)]
    y_peers = [lax.rem(y + d, 4) for d in range(1, 4)]

    locals_ = [
        pltpu.make_async_copy(cov_ref, flat, local_sem.at[0]),
        pltpu.make_async_copy(across_ref, head.at[0, SECTIONS : SECTIONS + grid_rows], local_sem.at[1]),
        pltpu.make_async_copy(along_ref, head.at[1, SECTIONS : SECTIONS + grid_rows], local_sem.at[2]),
        pltpu.make_async_copy(spread_ref, head.at[2, SECTIONS : SECTIONS + grid_rows], local_sem.at[3]),
        pltpu.make_async_copy(slab_ref, own, local_sem.at[4]),
    ]
    for copy in locals_:
        copy.start()

    barrier = pltpu.get_barrier_semaphore()
    peers = (
        [cells_device(after), cells_device(before)]
        + [cells_device(p * 4 + z_hi) for p in x_peers]
        + [cells_device(x * 4 + p) for p in z_peers]
        + [cols_device(z_lo * 8 + p * 2 + core) for p in y_peers]
        + [cols_device(z_lo * 8 + p * 2 + (1 - core)) for p in y_peers]
        + [cols_device((1 - z_lo) * 8 + y * 2 + core), cols_device(z_lo * 8 + y * 2 + (1 - core))]
    )
    for device in peers:
        pl.semaphore_signal(barrier, inc=1, device_id=device, device_id_type=MESH)

    for copy in locals_[:4]:
        copy.wait()
    for u in range(2):
        for i in range(grid_rows):
            head[3 + u, SECTIONS + i : SECTIONS + i + 1, :] = flat[u, :, i * width : (i + 1) * width]
    locals_[4].wait()
    part = 2 * width
    row_q = lax.broadcasted_iota(jnp.int32, (total, LANES), 0)
    wanted = jnp.zeros((total, LANES), jnp.int32)
    for u in range(2):
        for k in range(count):
            wanted = jnp.where(row_q == place(k) * 2 + u, cells_ref[u, k], wanted)
    wanted = jnp.concatenate([wanted] * (part // LANES), axis=1) - t * local_cells
    lane = lax.broadcasted_iota(jnp.int32, (total, part), 1)
    sub_8 = lax.broadcasted_iota(jnp.int32, (GROUP, part), 0)
    first_row = 2 * lax.rem(mine, 4)
    bf16 = jnp.bfloat16

    def pick(n, found):
        start = pl.multiple_of(n * part, part)
        chosen = jnp.where(lane + start == wanted, 1.0, 0.0).astype(bf16)
        rows = jnp.where(
            sub_8 == first_row,
            flat[0, :, pl.ds(start, part)],
            jnp.where(sub_8 == first_row + 1, flat[1, :, pl.ds(start, part)], 0.0),
        )
        block = jnp.concatenate([own[:, pl.ds(start, part)], rows, jnp.zeros_like(rows)], axis=0)
        upper = block.astype(bf16)
        rest = block - upper.astype(jnp.float32)
        middle = rest.astype(bf16)
        lower = (rest - middle.astype(jnp.float32)).astype(bf16)
        pieces = jnp.concatenate([upper, middle, lower], axis=0)
        return found + lax.dot_general(
            pieces, chosen, (((1,), (1,)), ((), ())), preferred_element_type=jnp.float32
        )

    height = columns + 2 * GROUP
    found = lax.fori_loop(
        0, local_cells // part, pick, jnp.zeros((3 * height, total), jnp.float32)
    )
    found = found[0:height] + found[height : 2 * height] + found[2 * height : 3 * height]
    found = jnp.concatenate([found, jnp.zeros((height, LANES - total), jnp.float32)], axis=1)
    rows = columns // 4
    packed = found[0:rows]
    for n in range(1, 4):
        packed = packed + pltpu.roll(found[n * rows : (n + 1) * rows], n * total, 1)
    msg_z[0:rows, :] = packed
    msg_z[rows : rows + GROUP, :] = found[columns : columns + GROUP]
    pl.semaphore_wait(barrier, len(peers))

    top = SECTIONS + grid_rows

    def halos(n):
        rows = pl.ds(pl.multiple_of(lax.div(n, 2) * GROUP, GROUP), GROUP)
        piece = edge // 2
        far = lax.rem(n, 2)
        above = pl.ds(pl.multiple_of(far * piece, piece), piece)
        below = pl.ds(pl.multiple_of((1 - far) * piece, piece), piece)
        last = pl.ds(pl.multiple_of(local_cells - edge + (1 - far) * piece, piece), piece)
        return (
            remote(
                slab_ref.at[rows, last], low.at[rows, below],
                halo_send.at[0, n], halo_recv.at[0, n], cells_device(after),
            ),
            remote(
                slab_ref.at[rows, above], high.at[rows, above],
                halo_send.at[1, n], halo_recv.at[1, n], cells_device(before),
            ),
        )

    quarter = pl.ds(pl.multiple_of(y * LANES, LANES), LANES)
    wind_rows = pl.ds(pl.multiple_of((1 - core) * (grid_rows - SECTIONS), SECTIONS), SECTIONS)
    side = lax.select(core == 0, after, before)
    winds = [
        remote(
            ref.at[wind_rows, quarter], head.at[n, pl.ds(pl.multiple_of(core * top, SECTIONS), SECTIONS), quarter],
            wind_send.at[n], wind_recv.at[n], cells_device(side),
        )
        for n, ref in enumerate((across_ref, along_ref, spread_ref))
    ]
    others = [(core, p) for p in y_peers] + [(1 - core, p) for p in y_peers] + [(1 - core, y)]

    def wind_copy(source, target):
        piece = head.at[
            0:3,
            pl.ds(pl.multiple_of(source[0] * top, SECTIONS), SECTIONS),
            pl.ds(pl.multiple_of(source[1] * LANES, LANES), LANES),
        ]
        return remote(
            piece, piece, w_send.at[target[0] * 4 + target[1]], w_recv.at[source[0] * 4 + source[1]],
            cols_device(z_lo * 8 + target[1] * 2 + target[0]),
        )

    z_copies = [
        remote(msg_z, slots_z.at[z_hi], z_send.at[p], z_recv.at[z_hi], cells_device(x * 4 + p)) for p in z_peers
    ]
    for copy in z_copies:
        copy.start()
    head_up = remote(
        head.at[3:5, grid_rows : grid_rows + SECTIONS, :], head.at[3:5, 0:SECTIONS, :],
        head_send.at[0], head_recv.at[0], cells_device(after),
    )
    head_down = remote(
        head.at[3:5, SECTIONS : 2 * SECTIONS, :], head.at[3:5, top : top + SECTIONS, :],
        head_send.at[1], head_recv.at[1], cells_device(before),
    )
    for copy in winds:
        copy.start()
    head_up.start()
    head_down.start()
    for n in range(FIRST):
        for copy in halos(n):
            copy.start()

    other = core * 8 + y * 2 + (1 - z_lo)
    span = 2 * grid_rows

    def block_of(position, blocks=1):
        return gathered.at[:, pl.ds(pl.multiple_of(position * span, span), blocks * span), :]

    def x_copy(slot, p):
        return remote(msg_x, slots_x.at[slot], x_send.at[p], x_recv.at[slot], cells_device(p * 4 + z_hi))

    def pair_copy(position):
        return remote(
            block_of(position), block_of(position), pair_send.at[0], pair_recv.at[0],
            cols_device((1 - z_lo) * 8 + y * 2 + core),
        )

    def pair_entries(slot):
        return remote(
            msg_c, slots_c.at[slot], pair_send.at[1], pair_recv.at[1],
            cols_device((1 - z_lo) * 8 + y * 2 + core),
        )

    def y_copy(source, p):
        both = block_of(core * 8 + source * 2, 2)
        return remote(both, both, y_send.at[p], y_recv.at[source], cols_device(z_lo * 8 + p * 2 + core))

    def core_copy(source):
        half = block_of(source * 8, 8)
        return remote(half, half, core_send, core_recv, cols_device(z_lo * 8 + y * 2 + (1 - core)))

    def entries_copy(source, target):
        mate = source[0] * 4 + source[1]
        two = slots_c.at[pl.ds(mate * 2, 2)]
        return remote(
            two, two, e_send.at[target[0] * 4 + target[1]], e_recv.at[mate],
            cols_device(z_lo * 8 + target[1] * 2 + target[0]),
        )

    def stencil(g, ranges):
        rows = pl.ds(pl.multiple_of(g * GROUP, GROUP), GROUP)

        def read(r, section):
            if section == 0:
                if r < SECTIONS:
                    return low[rows, r * width : (r + 1) * width]
                if r < top:
                    return own[rows, (r - SECTIONS) * width : (r - SECTIONS + 1) * width]
                return high[rows, (r - top) * width : (r - top + 1) * width]
            return (buf_a if section % 2 else buf_b)[r]

        for section in range(SECTIONS):
            for first, last in ranges(section):
                below, here = read(first - 1, section), read(first, section)
                for r in range(first, last):
                    above = read(r + 1, section)
                    new = (
                        coef[0, r] * here
                        + coef[1, r] * above
                        + coef[2, r] * below
                        + coef[3, r] * pltpu.roll(here, width - 1, 1)
                        + coef[4, r] * pltpu.roll(here, 1, 1)
                    )
                    if section == SECTIONS - 1:
                        result[rows, (r - SECTIONS) * width : (r - SECTIONS + 1) * width] = new
                    else:
                        (buf_b if section % 2 else buf_a)[r] = new
                    below, here = here, above

    def finish(g):
        rows = pl.ds(pl.multiple_of(g * GROUP, GROUP), GROUP)
        for i in range(grid_rows):
            part = slice(i * width, (i + 1) * width)
            result[rows, part] = result[rows, part] - corr[i, rows, :]

    def send_x():
        for p in z_peers:
            remote(msg_z, slots_z.at[p], z_send.at[p], z_recv.at[p], cells_device(x * 4 + p)).wait_recv()
        summed = msg_z[...]
        for p in z_peers:
            summed = summed + slots_z[p]
        msg_x[...] = summed
        for p in x_peers:
            x_copy(x, p).start()

    def forecast_cov():
        for source in others:
            wind_copy(source, source).wait_recv()
        head_up.wait_recv()
        head_down.wait_recv()
        half_across = 0.5 * head[0]
        half_along = 0.5 * head[1]
        spread = head[2]
        values = [
            1.0 - 4.0 * spread, spread - half_across, spread + half_across, spread - half_along, spread + half_along
        ]
        for n in range(5):
            natural[n] = values[n]

        def widen(r, carry):
            for n in range(5):
                coef[n, r] = jnp.broadcast_to(natural[n, pl.ds(r, 1), :], (GROUP, width))
            return carry

        lax.fori_loop(1, extent - 1, widen, 0)

        def cov_section(_, fields):
            new = []
            for f in fields:
                new.append(
                    values[0] * f
                    + values[1] * pltpu.roll(f, extent - 1, 0)
                    + values[2] * pltpu.roll(f, 1, 0)
                    + values[3] * pltpu.roll(f, width - 1, 1)
                    + values[4] * pltpu.roll(f, 1, 1)
                )
            return tuple(new)

        fields = lax.fori_loop(0, SECTIONS, cov_section, (head[3], head[4]))
        for u in range(2):
            rows = pl.ds(pl.multiple_of(mine * span + u * grid_rows, grid_rows), grid_rows)
            for v in range(width // LANES):
                gathered[v, rows, :] = fields[u][SECTIONS:top, v * LANES : (v + 1) * LANES]
        pair_copy(mine).start()

    def send_pair():
        for p in x_peers:
            x_copy(p, p).wait_recv()
        summed = msg_x[...]
        for p in x_peers:
            summed = summed + slots_x[p]
        quarter_rows = columns // 4
        picks = summed[0:quarter_rows]
        entries = summed[quarter_rows : quarter_rows + GROUP]
        lane = lax.broadcasted_iota(jnp.int32, (quarter_rows, LANES), 1)
        picks = [picks] + [pltpu.roll(picks, LANES - n * total, 1) for n in range(1, 4)]
        square = jnp.concatenate(
            [jnp.zeros((total, LANES), jnp.float32)]
            + [jnp.where(lane < total, block, 0.0) for block in picks]
            + [jnp.zeros((LANES - total - columns, LANES), jnp.float32)],
            axis=0,
        )
        right_side[...] = square.T[0:total, :]
        msg_c[...] = entries
        slots_c[mine] = entries
        pair_entries(mine).start()
        pair_copy(other).wait_recv()
        for p in y_peers:
            y_copy(y, p).start()

    def send_entries():
        pair_entries(other).wait_recv()
        for target in others:
            entries_copy((core, y), target).start()

    def send_core():
        for p in y_peers:
            y_copy(p, p).wait_recv()
        core_copy(core).start()

    def solve():
        for source in others:
            entries_copy(source, source).wait_recv()
        quarters = []
        for b in range(4):
            quarter = slots_c[4 * b]
            for n in range(1, 4):
                quarter = quarter + slots_c[4 * b + n]
            quarters.append(quarter)
        entries = jnp.concatenate(quarters, axis=0)
        turned = jnp.concatenate(
            [entries, jnp.zeros((LANES - total, LANES), jnp.float32)], axis=0
        ).T[0:total, :]
        row = lax.broadcasted_iota(jnp.int32, (total, LANES), 0)
        col = lax.broadcasted_iota(jnp.int32, (total, LANES), 1)
        row_u, col_u = jnp.bitwise_and(row, 1), jnp.bitwise_and(col, 1)
        system = jnp.where(
            row_u == col_u, 0.5 * (entries + turned), jnp.where(row_u < col_u, entries, turned)
        )
        noise = jnp.zeros((total, LANES), jnp.float32)
        for u in range(2):
            for k in range(count):
                noise = jnp.where(row == place(k) * 2 + u, noise_ref[u, k], noise)
        system = system + jnp.where(row == col, noise, 0.0)
        system = jnp.where(col < total, system, right_side[...])
        for u in range(2):
            for k in range(count):
                q = place(k) * 2 + u
                scaled = system[q : q + 1, :] / system[q : q + 1, q : q + 1]
                system = jnp.where(row == q, scaled, system - system[:, q : q + 1] * scaled)
        weights = jnp.concatenate(
            [system, jnp.zeros((LANES - total, LANES), jnp.float32)], axis=0
        ).T[total : total + columns, :]
        upper = weights.astype(jnp.bfloat16).astype(jnp.float32)
        lower = weights - upper
        weight[...] = (
            upper + pltpu.roll(upper, total, 1) + pltpu.roll(lower, 2 * total, 1) + pltpu.roll(lower, 3 * total, 1)
        )

    def correct():
        core_copy(1 - core).wait_recv()
        left = weight[...].astype(jnp.bfloat16)

        def one_row(i, carry):
            rows = jnp.concatenate(
                [gathered[v, pl.ds(i, total, stride=grid_rows), :] for v in range(width // LANES)], axis=1
            )
            upper = rows.astype(jnp.bfloat16)
            lower = (rows - upper.astype(jnp.float32)).astype(jnp.bfloat16)
            right = jnp.concatenate([upper, lower, upper, lower], axis=0)
            corr[i] = jnp.dot(left, right, preferred_element_type=jnp.float32)
            return carry

        lax.fori_loop(0, grid_rows, one_row, 0)

    near = SECTIONS // 2

    def begin(g):
        for copy in halos(2 * g):
            copy.wait_recv()
        stencil(g, lambda s: [(near + s + 1, extent - near - s - 1)])

    def end(g):
        for copy in halos(2 * g + 1):
            copy.wait_recv()
        stencil(g, lambda s: [(s + 1, near + s + 1), (extent - near - s - 1, extent - s - 1)])

    steps = 2 * groups

    def step(n, carry):
        @pl.when(lax.rem(n, 2) == 1)
        def _():
            begin(lax.div(n, 2))

        @pl.when(n < steps)
        def _():
            for copy in halos(n):
                copy.wait_send()

        @pl.when(n + AHEAD < steps)
        def _():
            for copy in halos(n + AHEAD):
                copy.start()

        @pl.when(n == STEP_HEAD)
        def _():
            forecast_cov()

        @pl.when(n == STEP_PAIR)
        def _():
            send_pair()

        @pl.when(n == STEP_Y)
        def _():
            send_entries()

        @pl.when(n == STEP_CORE)
        def _():
            send_core()
            solve()

        @pl.when(n == STEP_CORR)
        def _():
            correct()

        @pl.when(jnp.logical_and(n >= 2, lax.rem(n, 2) == 0))
        def _():
            end(lax.div(n, 2) - 1)

        @pl.when(n > STEP_END)
        def _():
            finish(2 * (n - STEP_END - 1))
            finish(2 * (n - STEP_END - 1) + 1)

        return carry

    for copy in winds:
        copy.wait_recv()
    for target in others:
        wind_copy((core, y), target).start()
    send_x()
    for n in range(FIRST, AHEAD):
        for copy in halos(n):
            copy.start()

    lax.fori_loop(0, steps + 1, step, 0)

    for copy in [head_up, head_down, pair_copy(mine), pair_entries(mine), core_copy(core)]:
        copy.wait_send()
    for copy in z_copies + winds:
        copy.wait_send()
    for p in x_peers:
        x_copy(x, p).wait_send()
    for p in y_peers:
        y_copy(y, p).wait_send()
    for target in others:
        entries_copy((core, y), target).wait_send()
        wind_copy((core, y), target).wait_send()


def local(
    slab_cols, observed_cov, observed_cells, noise_variance, wind_across, wind_along, diffusion
):
    columns, local_cells = slab_cols.shape
    grid_rows, width = wind_across.shape
    count = observed_cells.shape[1]
    total = 2 * count
    extent = grid_rows + 2 * SECTIONS
    edge = SECTIONS * width
    groups = columns // GROUP
    f32 = jnp.float32
    dma = pltpu.SemaphoreType.DMA
    any_space = pl.BlockSpec(memory_space=pltpu.HBM)
    scalars = pl.BlockSpec(memory_space=pltpu.SMEM)
    operands = [
        pltpu.with_memory_space_constraint(a, pltpu.HBM)
        for a in (
            observed_cells, noise_variance, slab_cols, observed_cov, wind_across, wind_along, diffusion
        )
    ]
    return pl.pallas_call(
        kernel,
        out_shape=pltpu.VMEM((columns, local_cells), f32),
        in_specs=[scalars, scalars] + [any_space] * 5,
        out_specs=pl.BlockSpec(memory_space=pltpu.VMEM),
        scratch_shapes=[
            pltpu.VMEM((columns, local_cells), f32),
            pltpu.VMEM((columns, edge), f32),
            pltpu.VMEM((columns, edge), f32),
            pltpu.VMEM((2, 1, local_cells), f32),
            pltpu.VMEM((5, extent, width), f32),
            pltpu.VMEM((5, extent, width), f32),
            pltpu.VMEM((5, extent, GROUP, width), f32),
            pltpu.VMEM((extent, GROUP, width), f32),
            pltpu.VMEM((extent, GROUP, width), f32),
            pltpu.VMEM((width // LANES, total * grid_rows, LANES), f32),
            pltpu.VMEM((grid_rows, columns, width), f32),
            pltpu.VMEM((columns, LANES), f32),
            pltpu.VMEM((total, LANES), f32),
            pltpu.VMEM((columns // 4 + GROUP, LANES), f32),
            pltpu.VMEM((4, columns // 4 + GROUP, LANES), f32),
            pltpu.VMEM((columns // 4 + GROUP, LANES), f32),
            pltpu.VMEM((4, columns // 4 + GROUP, LANES), f32),
            pltpu.VMEM((GROUP, LANES), f32),
            pltpu.VMEM((16, GROUP, LANES), f32),
            dma((5,)),
            dma((2, 2 * groups)),
            dma((2, 2 * groups)),
            dma((2,)),
            dma((2,)),
            dma((3,)),
            dma((3,)),
            dma((8,)),
            dma((8,)),
            dma((4,)),
            dma((4,)),
            dma((4,)),
            dma((4,)),
            dma((8,)),
            dma((8,)),
            dma((2,)),
            dma((2,)),
            dma((4,)),
            dma((4,)),
            dma,
            dma,
        ],
        compiler_params=pltpu.CompilerParams(
            collective_id=0, has_side_effects=True, vmem_limit_bytes=32 * 1024 * 1024
        ),
    )(*operands)


def solution(mesh):
    return jax.shard_map(
        local,
        mesh=mesh,
        in_specs=(
            P("cols", "cells"),
            P(None, "cols", "cells"),
            P(),
            P(),
            P("cells", None),
            P("cells", None),
            P("cells", None),
        ),
        out_specs=P("cols", "cells"),
        check_vma=False,
    )
```
